512 devices in a mesh: rep: 16 (over z, core), tp: 32 (over y, x).
Axes of the slice: x: 4, y: 8, z: 8, core: 2. Of those that a mesh axis runs over, the one named last changes fastest.
Arguments:
- queries: bfloat16 [2048, 4096], P(('rep', 'tp')), parts along dimension 0, may hold values from -18 to 18
- key_cache: bfloat16 [2048, 256, 512], P(('rep', 'tp')), parts along dimension 0, may hold values from -6 to 6
- value_cache: bfloat16 [2048, 256, 512], P(('rep', 'tp')), parts along dimension 0, may hold values from -24 to 24
- lengths: int32 [2048], P(('rep', 'tp')), parts along dimension 0, may hold values from 32 to 256, as said below
- request_adapter: int32 [2048], P('rep'), parts along dimension 0, may hold values from 0 to 199, as said below
- block_adapter: int32 [256], P('rep'), parts along dimension 0, may hold values from 0 to 199, as said below
- output_weight: bfloat16 [4096, 8192], P('tp'), may hold values from -0.1875 to 0.1875
- down_factors: bfloat16 [256, 4096, 64], P('rep', 'tp'), parts along dimension 0, may hold values from -0.09375 to 0.09375
- up_factors: bfloat16 [256, 64, 8192], P('rep', None, 'tp'), parts along dimension 0, may hold values from -0.75 to 0.75
Outputs:
- layer_out: bfloat16 [2048, 8192], P('rep', 'tp'), parts along dimension 0
The draws below stay inside these ranges and needn't reach their ends.
There are 16 independent parts, one for each index of `rep`. The reference program is written for one: setup_inputs(seed, part) draws one part's arguments, and reference() takes and returns one part's arrays. A program takes and returns all parts, laid end to end along the dimension named above; an argument that names none is the same for every part. Nothing has to cross between parts.
Inputs may be any that keep to these rules, and one draw needn't show every extreme that they name: `lengths`: every request has live positions; some request's cache is live at all 256 positions. `block_adapter`: the entries are distinct adapters. `request_adapter`: every request's adapter appears in block_adapter; block b takes the requests whose adapter is block_adapter[b], at most 16 of them, and some block takes exactly 16.
All inputs are finite; a program needn't handle non-finite values.
Results may differ from the reference program's by a relative error of at most 0.006.
Values may be sent and summed in bfloat16 or wider, within the bound.
No kernel may reach another device: no remote copies, remote signals or barrier semaphores. Data moves between devices by JAX's collectives and lax.ppermute only.
A program may use at most 64 MiB of HBM per device.

```python
import math
import jax
import jax.numpy as jnp
from jax import lax

MODEL_WIDTH = 8192
HEAD_SIZE = 128
QUERY_HEADS = 32
KVH = 4
ADAPTER_RANK = 64
BLK = 16
ADAPTERS = 200
CTX = 256
GROUP_REQUESTS = 128
PADDED_BLOCKS = 16


def route_plan(key):
    half_block = BLK // 2
    pair_count = PADDED_BLOCKS // 2
    swings = jax.random.randint(jax.random.fold_in(key, 21), (pair_count,), 0, half_block)
    swings = jnp.where(jnp.arange(pair_count) == 0, half_block, swings)
    fill_counts = jnp.stack([half_block + swings, half_block - swings], axis=1).reshape(PADDED_BLOCKS)
    fill_counts = fill_counts[jax.random.permutation(jax.random.fold_in(key, 22), PADDED_BLOCKS)]
    resident = jax.random.permutation(jax.random.fold_in(key, 23), ADAPTERS)[:PADDED_BLOCKS].astype(jnp.int32)
    fill_ends = jnp.cumsum(fill_counts)
    positions = jnp.arange(GROUP_REQUESTS)
    block_of = jnp.sum((fill_ends[None, :] <= positions[:, None]).astype(jnp.int32), axis=1)
    in_order = resident[block_of]
    shuffled = jax.random.permutation(jax.random.fold_in(key, 24), GROUP_REQUESTS)
    return (in_order[shuffled].astype(jnp.int32), resident)


def draw_queries(key, part):
    key = jax.random.fold_in(key, 5)
    return jnp.clip(jax.random.normal(key, (GROUP_REQUESTS, QUERY_HEADS * HEAD_SIZE), jnp.float32), -6.0, 6.0).astype(jnp.bfloat16)


def draw_key_cache(key, part):
    key = jax.random.fold_in(key, 3)
    return jnp.clip(jax.random.normal(key, (GROUP_REQUESTS, CTX, KVH * HEAD_SIZE), jnp.float32), -6.0, 6.0).astype(jnp.bfloat16)


def draw_lengths(key, part):
    key = jax.random.fold_in(key, 7)
    drawn = jax.random.randint(key, (GROUP_REQUESTS,), CTX // 8, CTX + 1)
    longest = jax.random.randint(jax.random.fold_in(key, 1), (), 0, GROUP_REQUESTS)
    return jnp.where(jnp.arange(GROUP_REQUESTS) == longest, CTX, drawn).astype(jnp.int32)


def draw_request_adapter(key, part):
    request_ids, resident = route_plan(key)
    return request_ids


def draw_block_adapter(key, part):
    request_ids, resident = route_plan(key)
    return resident


def with_spikes(array, stream_key, source, target, blocks, factor):
    def block_of(axis_at):
        return (jnp.arange(array.shape[axis_at]) // (array.shape[axis_at] // blocks)).reshape((-1,) + (1,) * (array.ndim - 1 - axis_at))

    one_side = jax.random.permutation(stream_key, blocks)[block_of(target)]
    second = (block_of(target) + blocks // 2) % blocks
    return jnp.where((block_of(source) == one_side) | (block_of(source) == second), factor * array, array)


def steps_of(stream_key, dims, pieces, least, largest):
    def one(dim, blocks):
        steps = jax.random.uniform(jax.random.fold_in(jax.random.fold_in(stream_key, 6), dim), (blocks,), jnp.float32, least / len(pieces), largest / len(pieces))
        return jnp.repeat(jnp.exp(steps), dims[dim] // blocks).reshape((-1,) + (1,) * (len(dims) - dim - 1))

    level = one(*pieces[0])
    for cut in pieces[1:]:
        level = level * one(*cut)
    return level


def gaussian(stream_key, extent, spread, most, split=(), kind=jnp.bfloat16):
    factor_of = steps_of(stream_key, extent, split, -0.22, 0.18) if split else 1.0
    result = jax.random.normal(stream_key, extent, jnp.float32) * spread * factor_of
    return jnp.minimum(jnp.maximum(result, -most), most).astype(kind)


def bell_draw_with(own_key, extent, width, reach, split, heavy, kind=jnp.bfloat16):
    values = width * jax.random.normal(own_key, extent, jnp.float32)
    if split:
        values = values * steps_of(own_key, extent, split, -0.22, 0.18)
    return jnp.clip(with_spikes(values, jax.random.fold_in(own_key, 3), *heavy), -reach, reach).astype(kind)


def setup_inputs(seed: int = 0, part: int = 0) -> dict:
    seeds = jax.random.split(jax.random.key(seed), 10)
    own_keys = jax.random.split(jax.random.fold_in(seeds[9], part), 10)
    queries = draw_queries(jax.random.fold_in(jax.random.fold_in(seeds[9], part), 71), part)
    key_cache = draw_key_cache(jax.random.fold_in(jax.random.fold_in(seeds[9], part), 71), part)
    value_cache = gaussian(own_keys[2], (GROUP_REQUESTS, CTX, KVH * HEAD_SIZE), 4.0, 24.0, ((0, 32),))
    lengths = draw_lengths(jax.random.fold_in(jax.random.fold_in(seeds[9], part), 71), part)
    request_adapter = draw_request_adapter(jax.random.fold_in(jax.random.fold_in(seeds[9], part), 71), part)
    block_adapter = draw_block_adapter(jax.random.fold_in(jax.random.fold_in(seeds[9], part), 71), part)
    output_weight = bell_draw_with(seeds[6], (QUERY_HEADS * HEAD_SIZE, MODEL_WIDTH), (QUERY_HEADS * HEAD_SIZE) ** -0.5, 0.1875, ((0, 32),), (0, 1, 32, 2.75))
    down_factors = gaussian(own_keys[7], (PADDED_BLOCKS, QUERY_HEADS * HEAD_SIZE, ADAPTER_RANK), (QUERY_HEADS * HEAD_SIZE) ** -0.5, 0.09375, ((1, 32),))
    up_factors = gaussian(own_keys[8], (PADDED_BLOCKS, ADAPTER_RANK, MODEL_WIDTH), ADAPTER_RANK ** -0.5, 0.75, ((2, 32),))
    return dict(queries=queries, key_cache=key_cache, value_cache=value_cache, lengths=lengths, request_adapter=request_adapter, block_adapter=block_adapter, output_weight=output_weight, down_factors=down_factors, up_factors=up_factors)


def attend(queries, key_cache, value_cache, lengths):
    row_count = queries.shape[0]
    group_size = QUERY_HEADS // KVH
    query_split = queries.astype(jnp.float32).reshape(row_count, KVH, group_size, HEAD_SIZE)
    key_split = key_cache.astype(jnp.float32).reshape(row_count, CTX, KVH, HEAD_SIZE)
    value_split = value_cache.astype(jnp.float32).reshape(row_count, CTX, KVH, HEAD_SIZE)
    scores = jnp.einsum('rkgd,rpkd->rkgp', query_split, key_split) / math.sqrt(HEAD_SIZE)
    live_keys = (jnp.arange(CTX, dtype=jnp.int32)[None, :] < lengths[:, None])[:, None, None, :]
    scores = jnp.where(live_keys, scores, -1e+30)
    row_max = lax.optimization_barrier(jnp.max(scores, axis=-1, keepdims=True))
    raw_weights = jnp.where(live_keys, jnp.exp(scores - row_max), 0.0)
    weights = (raw_weights / lax.optimization_barrier(jnp.sum(raw_weights, axis=-1, keepdims=True))).astype(jnp.bfloat16)
    attended = jnp.einsum('rkgp,rpkd->rkgd', weights.astype(jnp.float32), value_split)
    return attended.reshape(row_count, QUERY_HEADS * HEAD_SIZE).astype(jnp.bfloat16)

def reference(queries, key_cache, value_cache, lengths, request_adapter, block_adapter, output_weight, down_factors, up_factors):
    head_output = attend(queries, key_cache, value_cache, lengths)
    base_output = jnp.dot(head_output, output_weight, preferred_element_type=jnp.float32)
    block_indices = jnp.arange(PADDED_BLOCKS, dtype=jnp.int32)

    def shrink_step(running, current_block):
        block_contribution = jnp.dot(head_output, down_factors[current_block], preferred_element_type=jnp.float32)
        matches = (request_adapter == block_adapter[current_block])[:, None]
        return (running + jnp.where(matches, block_contribution, 0.0), None)
    shrink, unused_value = lax.scan(shrink_step, jnp.zeros((GROUP_REQUESTS, ADAPTER_RANK), jnp.float32), block_indices)
    reduced_activations = shrink.astype(jnp.bfloat16)

    def upward_product(running, current_block):
        block_contribution = jnp.dot(reduced_activations, up_factors[current_block], preferred_element_type=jnp.float32)
        matches = (request_adapter == block_adapter[current_block])[:, None]
        return (running + jnp.where(matches, block_contribution, 0.0), None)
    adapter_output, unused_value = lax.scan(upward_product, jnp.zeros((GROUP_REQUESTS, MODEL_WIDTH), jnp.float32), block_indices)
    return (base_output + adapter_output).astype(jnp.bfloat16)
```

```python
import functools
import math

import jax
import jax.numpy as jnp
from jax import lax
from jax.experimental import pallas as pl
from jax.experimental.pallas import tpu as pltpu
from jax.sharding import PartitionSpec as P

HEAD_SIZE = 128
QUERY_HEADS = 32
KVH = 4
CTX = 256
BF16, F32 = jnp.bfloat16, jnp.float32
VMEM_LIMIT = 32 * 1024 * 1024


def attend_kernel(len_ref, q_ref, k_hbm, v_hbm, out_ref, k_buf, v_buf, k_sem, v_sem):
    rows = q_ref.shape[0]
    group = QUERY_HEADS // KVH
    k_copies = [pltpu.make_async_copy(k_hbm.at[r], k_buf.at[r], k_sem.at[r]) for r in range(rows)]
    v_copies = [pltpu.make_async_copy(v_hbm.at[r], v_buf.at[r], v_sem.at[r]) for r in range(rows)]
    for r in range(rows):
        k_copies[r].start()
        v_copies[r].start()
    head_row = lax.broadcasted_iota(jnp.int32, (QUERY_HEADS, HEAD_SIZE), 0) // group
    position = lax.broadcasted_iota(jnp.int32, (QUERY_HEADS, CTX), 1)
    for r in range(rows):
        q = q_ref[r]
        spread = jnp.concatenate(
            [jnp.where(head_row == k, q, jnp.zeros_like(q)) for k in range(KVH)], axis=1
        )
        k_copies[r].wait()
        scores = lax.dot_general(
            spread, k_buf[r], (((1,), (1,)), ((), ())), preferred_element_type=F32
        ) * (1.0 / math.sqrt(HEAD_SIZE))
        live = position < len_ref[r]
        scores = jnp.where(live, scores, -1e30)
        raw = jnp.where(live, jnp.exp(scores - jnp.max(scores, axis=1, keepdims=True)), 0.0)
        probs = (raw / jnp.sum(raw, axis=1, keepdims=True)).astype(BF16)
        v_copies[r].wait()
        wide = jnp.dot(probs, v_buf[r], preferred_element_type=F32)
        out_ref[r] = jnp.concatenate(
            [
                wide[k * group : (k + 1) * group, k * HEAD_SIZE : (k + 1) * HEAD_SIZE]
                for k in range(KVH)
            ],
            axis=0,
        ).astype(BF16)


def attend(queries, key_cache, value_cache, lengths):
    rows = queries.shape[0]
    return pl.pallas_call(
        attend_kernel,
        out_shape=jax.ShapeDtypeStruct((rows, QUERY_HEADS, HEAD_SIZE), BF16),
        in_specs=[
            pl.BlockSpec(memory_space=pltpu.SMEM),
            pl.BlockSpec(memory_space=pltpu.VMEM),
            pl.BlockSpec(memory_space=pl.ANY),
            pl.BlockSpec(memory_space=pl.ANY),
        ],
        out_specs=pl.BlockSpec(memory_space=pltpu.VMEM),
        scratch_shapes=[
            pltpu.VMEM((rows, CTX, KVH * HEAD_SIZE), BF16),
            pltpu.VMEM((rows, CTX, KVH * HEAD_SIZE), BF16),
            pltpu.SemaphoreType.DMA((rows,)),
            pltpu.SemaphoreType.DMA((rows,)),
        ],
        compiler_params=pltpu.CompilerParams(vmem_limit_bytes=VMEM_LIMIT),
        name="attend",
    )(lengths, queries.reshape(rows, QUERY_HEADS, HEAD_SIZE), key_cache, value_cache)


def project_kernel(block_ref, adapter_ref, heads_ref, weight_ref, down_ref, out_ref):
    devices, _, width = out_ref.shape
    rows = heads_ref.shape[0]
    heads = heads_ref[...]
    adapter = adapter_ref[...]
    for d in range(devices):
        out_ref[d, :rows, :] = jnp.dot(
            heads, weight_ref[:, d * width : (d + 1) * width], preferred_element_type=F32
        ).astype(BF16)
    shrink = jnp.zeros((rows, down_ref.shape[2]), F32)
    for b in range(down_ref.shape[0]):
        mine = jnp.where(adapter == block_ref[b], heads, jnp.zeros_like(heads))
        shrink += jnp.dot(mine, down_ref[b], preferred_element_type=F32)
    quarter = rows * shrink.shape[1] // width
    packed = jnp.concatenate(
        [shrink[i * quarter : (i + 1) * quarter] for i in range(rows // quarter)], axis=1
    ).astype(BF16)
    for d in range(devices):
        out_ref[d, rows:, :] = packed


def project(heads, weight, down, adapter_col, block_adapter, devices):
    rows = heads.shape[0]
    width = weight.shape[1] // devices
    extra = rows * down.shape[2] // width
    vmem = pl.BlockSpec(memory_space=pltpu.VMEM)
    return pl.pallas_call(
        project_kernel,
        out_shape=jax.ShapeDtypeStruct((devices, rows + extra, width), BF16),
        in_specs=[pl.BlockSpec(memory_space=pltpu.SMEM)] + [vmem] * 4,
        out_specs=vmem,
        compiler_params=pltpu.CompilerParams(vmem_limit_bytes=VMEM_LIMIT),
        name="project",
    )(block_adapter, adapter_col, heads, weight, down)


def finish_kernel(block_ref, adapter_ref, parts_ref, up_ref, out_ref):
    count = parts_ref.shape[0]
    rows, width = out_ref.shape
    blocks, rank, _ = up_ref.shape
    packed = parts_ref[0, rows:, :].astype(F32)
    for s in range(1, count):
        packed += parts_ref[s, rows:, :].astype(F32)
    low_rank = jnp.concatenate(
        [packed[:, i * rank : (i + 1) * rank] for i in range(width // rank)], axis=0
    ).astype(BF16)
    adapter = adapter_ref[...]
    spread = jnp.concatenate(
        [
            jnp.where(adapter == block_ref[b], low_rank, jnp.zeros_like(low_rank))
            for b in range(blocks)
        ],
        axis=1,
    )
    lora = jnp.dot(
        spread, up_ref[...].reshape(blocks * rank, width), preferred_element_type=F32
    )
    step = 32
    for i in range(0, rows, step):
        total = parts_ref[0, i : i + step, :].astype(F32)
        for s in range(1, count):
            total += parts_ref[s, i : i + step, :].astype(F32)
        out_ref[i : i + step, :] = (total + lora[i : i + step]).astype(BF16)


def finish(parts, up, adapter_col, block_adapter, rows):
    width = parts.shape[2]
    vmem = pl.BlockSpec(memory_space=pltpu.VMEM)
    return pl.pallas_call(
        finish_kernel,
        out_shape=jax.ShapeDtypeStruct((rows, width), BF16),
        in_specs=[pl.BlockSpec(memory_space=pltpu.SMEM)] + [vmem] * 3,
        out_specs=vmem,
        compiler_params=pltpu.CompilerParams(vmem_limit_bytes=VMEM_LIMIT),
        name="finish",
    )(block_adapter, adapter_col, parts, up)


def per_device(
    devices,
    queries,
    key_cache,
    value_cache,
    lengths,
    request_adapter,
    block_adapter,
    output_weight,
    down_factors,
    up_factors,
):
    adapter_col = request_adapter[:, None]
    rows = request_adapter.shape[0]
    own = attend(queries, key_cache, value_cache, lengths)
    heads = lax.all_to_all(own, "tp", split_axis=1, concat_axis=0, tiled=True)
    heads = heads.reshape(rows, HEAD_SIZE)
    parts = project(heads, output_weight, down_factors, adapter_col, block_adapter, devices)
    parts = lax.all_to_all(parts, "tp", split_axis=0, concat_axis=0, tiled=True)
    return finish(parts, up_factors, adapter_col, block_adapter, rows)


def solution(mesh):
    in_specs = (
        P(("rep", "tp"), None),
        P(("rep", "tp"), None, None),
        P(("rep", "tp"), None, None),
        P(("rep", "tp")),
        P("rep"),
        P("rep"),
        P("tp", None),
        P("rep", "tp", None),
        P("rep", None, "tp"),
    )
    return jax.shard_map(
        functools.partial(per_device, mesh.shape["tp"]),
        mesh=mesh,
        in_specs=in_specs,
        out_specs=P("rep", "tp"),
        check_vma=False,
    )
```

```python
import functools
import math

import jax
import jax.numpy as jnp
from jax import lax
from jax.experimental import pallas as pl
from jax.experimental.pallas import tpu as pltpu
from jax.sharding import PartitionSpec as P

HEAD_SIZE = 128
QUERY_HEADS = 32
KVH = 4
CTX = 256
QUAD = 4
LINE = 256
BF16, F32 = jnp.bfloat16, jnp.float32
VMEM = pl.BlockSpec(memory_space=pltpu.VMEM)
SMEM = pl.BlockSpec(memory_space=pltpu.SMEM)
HBM = pl.BlockSpec(memory_space=pl.ANY)
PARAMS = pltpu.CompilerParams(vmem_limit_bytes=32 * 1024 * 1024)


def regroup_kernel(quad_ref, weight_hbm, *refs):
    outs, sem = refs[:QUAD], refs[QUAD]
    lines = outs[0].shape[1] // LINE
    copies = []
    for ahead, out_ref in enumerate(outs):
        x = lax.rem(quad_ref[0] + ahead, QUAD)
        for y in range(lines):
            start = pl.multiple_of((y * QUAD + x) * LINE, LINE)
            copies.append(
                pltpu.make_async_copy(
                    weight_hbm.at[:, pl.ds(start, LINE)],
                    out_ref.at[:, pl.ds(y * LINE, LINE)],
                    sem.at[ahead, y],
                )
            )
    for copy in copies:
        copy.start()
    for copy in copies:
        copy.wait()


def regroup(quad, weight):
    depth, columns = weight.shape
    piece = jax.ShapeDtypeStruct((depth, columns // QUAD), BF16)
    return pl.pallas_call(
        regroup_kernel,
        out_shape=(piece,) * QUAD,
        in_specs=[SMEM, HBM],
        out_specs=(VMEM,) * QUAD,
        scratch_shapes=[pltpu.SemaphoreType.DMA((QUAD, columns // QUAD // LINE))],
        compiler_params=PARAMS,
        name="regroup",
    )(quad, weight)


def attend_kernel(len_ref, q_ref, k_ref, v_ref, out_ref):
    rows = q_ref.shape[0]
    group = QUERY_HEADS // KVH
    head_row = lax.broadcasted_iota(jnp.int32, (QUERY_HEADS, HEAD_SIZE), 0) // group
    position = lax.broadcasted_iota(jnp.int32, (QUERY_HEADS, CTX), 1)
    attended = []
    for r in range(rows):
        q = q_ref[r]
        spread = jnp.concatenate(
            [jnp.where(head_row == k, q, jnp.zeros_like(q)) for k in range(KVH)], axis=1
        )
        scores = lax.dot_general(
            spread, k_ref[r], (((1,), (1,)), ((), ())), preferred_element_type=F32
        ) * (1.0 / math.sqrt(HEAD_SIZE))
        live = position < len_ref[r]
        scores = jnp.where(live, scores, -1e30)
        raw = jnp.where(live, jnp.exp(scores - jnp.max(scores, axis=1, keepdims=True)), 0.0)
        probs = (raw / jnp.sum(raw, axis=1, keepdims=True)).astype(BF16)
        wide = jnp.dot(probs, v_ref[r], preferred_element_type=F32)
        attended.append(
            jnp.concatenate(
                [
                    wide[k * group : (k + 1) * group, k * HEAD_SIZE : (k + 1) * HEAD_SIZE]
                    for k in range(KVH)
                ],
                axis=0,
            )
        )
    stacked = jnp.stack(attended, axis=1)
    for y in range(QUERY_HEADS // QUAD):
        piece = stacked[y * QUAD : (y + 1) * QUAD].reshape(QUAD * rows, HEAD_SIZE).astype(BF16)
        for x in range(QUAD):
            out_ref[y * QUAD + x] = piece


def attend(queries, key_cache, value_cache, lengths):
    rows = queries.shape[0]
    return pl.pallas_call(
        attend_kernel,
        out_shape=jax.ShapeDtypeStruct((QUERY_HEADS, QUAD * rows, HEAD_SIZE), BF16),
        in_specs=[SMEM, VMEM, VMEM, VMEM],
        out_specs=VMEM,
        compiler_params=PARAMS,
        name="attend",
    )(lengths, queries.reshape(rows, QUERY_HEADS, HEAD_SIZE), key_cache, value_cache)


def pick_rows(spans, index):
    count, size = spans.shape
    rows = count // QUAD
    row = lax.broadcasted_iota(jnp.int32, (rows, count), 0)
    column = lax.broadcasted_iota(jnp.int32, (rows, count), 1)
    wanted = (row // 4) * 16 + index * 4 + row % 4
    choice = jnp.where(column == wanted, 1.0, 0.0).astype(BF16)
    return jnp.dot(choice, spans, preferred_element_type=F32).astype(BF16)


def shrink_kernel(quad_ref, block_ref, adapter_ref, spans_ref, down_ref, out_ref):
    devices, half, _ = out_ref.shape
    heads = pick_rows(spans_ref[...], quad_ref[0])
    adapter = adapter_ref[...]
    rank = down_ref.shape[1]
    shrink = jnp.zeros((heads.shape[0], rank), F32)
    for b in range(down_ref.shape[0]):
        mine = jnp.where(adapter == block_ref[b], heads, jnp.zeros_like(heads))
        shrink += lax.dot_general(
            mine, down_ref[b], (((1,), (1,)), ((), ())), preferred_element_type=F32
        )
    for y in range(devices // QUAD):
        base = y * 2 * half
        pair = jnp.concatenate(
            [shrink[base : base + half], shrink[base + half : base + 2 * half]], axis=1
        ).astype(BF16)
        for x in range(QUAD):
            out_ref[y * QUAD + x] = pair


def shrink_parts(quad, spans, down, adapter_col, block_adapter):
    devices = spans.shape[0] // (QUAD * 4)
    rows = spans.shape[0] // QUAD
    half = rows // (devices // QUAD) // 2
    return pl.pallas_call(
        shrink_kernel,
        out_shape=jax.ShapeDtypeStruct((devices, half, 2 * down.shape[2]), BF16),
        in_specs=[SMEM, SMEM, VMEM, VMEM, VMEM],
        out_specs=VMEM,
        compiler_params=PARAMS,
        name="shrink",
    )(quad, block_adapter, adapter_col, spans, jnp.swapaxes(down, 1, 2))


def project_kernel(quad_ref, spans_ref, *refs):
    weight_refs, shrink_ref, out_ref = refs[:QUAD], refs[QUAD], refs[QUAD + 1]
    dests, _, width = out_ref.shape
    rows = spans_ref.shape[0] // QUAD
    spans = spans_ref[...]
    heads = jnp.concatenate(
        [pick_rows(spans, lax.rem(quad_ref[0] + QUAD - ahead, QUAD)) for ahead in range(QUAD)],
        axis=1,
    )
    for d in range(dests):
        columns = jnp.concatenate(
            [ref[:, d * width : (d + 1) * width] for ref in weight_refs], axis=0
        )
        out_ref[d, :rows, :] = jnp.dot(heads, columns, preferred_element_type=F32).astype(BF16)
    low_rank = shrink_ref[0].astype(F32)
    for s in range(1, shrink_ref.shape[0]):
        low_rank += shrink_ref[s].astype(F32)
    wide = jnp.concatenate([low_rank, jnp.zeros_like(low_rank)], axis=1)
    block = jnp.concatenate([wide, jnp.zeros_like(wide)], axis=0).astype(BF16)
    for d in range(dests):
        out_ref[d, rows:, :] = block


def project(quad, spans, weights, shrinks):
    rows = spans.shape[0] // QUAD
    dests = weights[0].shape[1] // LINE
    return pl.pallas_call(
        project_kernel,
        out_shape=jax.ShapeDtypeStruct((dests, rows + 2 * shrinks.shape[1], LINE), BF16),
        in_specs=[SMEM] + [VMEM] * (QUAD + 2),
        out_specs=VMEM,
        compiler_params=PARAMS,
        name="project",
    )(quad, spans, *weights, shrinks)


def finish_kernel(block_ref, adapter_ref, parts_ref, up_ref, out_ref):
    count = parts_ref.shape[0]
    rows, width = out_ref.shape
    blocks, rank, _ = up_ref.shape
    lanes = 2 * rank
    half = rows // count // 2
    left = lax.broadcasted_iota(jnp.int32, (half, lanes), 1) < rank
    pieces = []
    for s in range(count):
        pair = parts_ref[s, rows : rows + 2 * half, :lanes].astype(F32)[:half]
        turned = jnp.concatenate([pair[:, rank:], pair[:, :rank]], axis=1)
        pieces += [jnp.where(left, pair, turned), jnp.where(left, turned, pair)]
    low_rank = jnp.concatenate(pieces, axis=0)
    adapter = adapter_ref[...]
    wide_left = lax.broadcasted_iota(jnp.int32, (rows, lanes), 1) < rank
    spread = []
    for b in range(0, blocks, 2):
        match = jnp.where(wide_left, block_ref[b], block_ref[b + 1]) == adapter
        spread.append(jnp.where(match, low_rank, 0.0).astype(BF16))
    lora = jnp.dot(
        jnp.concatenate(spread, axis=1),
        up_ref[...].reshape(blocks * rank, width),
        preferred_element_type=F32,
    )
    total = parts_ref[0, :rows, :].astype(F32)
    for s in range(1, count):
        total += parts_ref[s, :rows, :].astype(F32)
    out_ref[...] = (total + lora).astype(BF16)


def finish(parts, up, adapter_col, block_adapter, rows):
    return pl.pallas_call(
        finish_kernel,
        out_shape=jax.ShapeDtypeStruct((rows, parts.shape[2]), BF16),
        in_specs=[SMEM, VMEM, VMEM, VMEM],
        out_specs=VMEM,
        compiler_params=PARAMS,
        name="finish",
    )(block_adapter, adapter_col, parts, up)


def per_device(
    devices,
    queries,
    key_cache,
    value_cache,
    lengths,
    request_adapter,
    block_adapter,
    output_weight,
    down_factors,
    up_factors,
):
    lines = devices // QUAD
    along_y = [[y * QUAD + x for y in range(lines)] for x in range(QUAD)]
    exchange = functools.partial(
        lax.all_to_all, axis_name="tp", split_axis=0, concat_axis=0, tiled=True
    )
    rows = request_adapter.shape[0]
    adapter_col = request_adapter[:, None]
    quad = (lax.axis_index("tp") & (QUAD - 1)).astype(jnp.int32)[None]

    weights = list(regroup(quad, output_weight))
    for ahead in range(1, QUAD):
        turn = [
            (y * QUAD + x, y * QUAD + (x + ahead) % QUAD) for y in range(lines) for x in range(QUAD)
        ]
        weights[ahead] = lax.ppermute(weights[ahead], "tp", turn)
    spans = exchange(attend(queries, key_cache, value_cache, lengths))
    spans = spans.reshape(QUAD * rows, HEAD_SIZE)
    shrinks = exchange(shrink_parts(quad, spans, down_factors, adapter_col, block_adapter))
    parts = exchange(project(quad, spans, weights, shrinks), axis_index_groups=along_y)
    return finish(parts, up_factors, adapter_col, block_adapter, rows)


def solution(mesh):
    in_specs = (
        P(("rep", "tp"), None),
        P(("rep", "tp"), None, None),
        P(("rep", "tp"), None, None),
        P(("rep", "tp")),
        P("rep"),
        P("rep"),
        P("tp", None),
        P("rep", "tp", None),
        P("rep", None, "tp"),
    )
    return jax.shard_map(
        functools.partial(per_device, mesh.shape["tp"]),
        mesh=mesh,
        in_specs=in_specs,
        out_specs=P("rep", "tp"),
        check_vma=False,
    )
```

```python
import functools
import math

import jax
import jax.numpy as jnp
from jax import lax
from jax.experimental import pallas as pl
from jax.experimental.pallas import tpu as pltpu
from jax.sharding import PartitionSpec as P

HEAD_SIZE = 128
QUERY_HEADS = 32
KVH = 4
CTX = 256
QUAD = 4
LINE = 256
BF16, F32 = jnp.bfloat16, jnp.float32
VMEM = pl.BlockSpec(memory_space=pltpu.VMEM)
SMEM = pl.BlockSpec(memory_space=pltpu.SMEM)
HBM = pl.BlockSpec(memory_space=pltpu.HBM)
PARAMS = pltpu.CompilerParams(vmem_limit_bytes=32 * 1024 * 1024)


def in_quad(q, m):
    return ((q >> 1) * 2 + (m >> 1)) * 4 + (q & 1) * 2 + (m & 1)


def start_kernel(
    member_ref, len_ref, q_ref, k_hbm, v_hbm, w_hbm, heads_ref, *refs
):
    pieces = refs[: QUAD - 1]
    k_buf, v_buf, k_sem, v_sem, w_sem = refs[QUAD - 1 :]
    rows, size = k_buf.shape[0], HEAD_SIZE
    k_copies = [pltpu.make_async_copy(k_hbm.at[r], k_buf.at[r], k_sem.at[r]) for r in range(rows)]
    v_copies = [pltpu.make_async_copy(v_hbm.at[r], v_buf.at[r], v_sem.at[r]) for r in range(rows)]
    w_copies = []
    for step, piece in enumerate(pieces):
        place = in_quad(0, lax.bitwise_xor(member_ref[0], step + 1))
        for q in range(piece.shape[1] // LINE):
            first = pl.multiple_of((in_quad(q, 0) + place) * LINE, LINE)
            w_copies.append(
                pltpu.make_async_copy(
                    w_hbm.at[:, pl.ds(first, LINE)],
                    piece.at[:, pl.ds(q * LINE, LINE)],
                    w_sem.at[step, q],
                )
            )
    for copy in k_copies + v_copies + w_copies:
        copy.start()

    q = q_ref[...].astype(F32)
    q_rows = jnp.concatenate(
        [q[:, h * size : (h + 1) * size] for h in range(QUERY_HEADS)], axis=0
    )
    q_lanes = q_rows.T.astype(BF16)
    count = rows * QUERY_HEADS
    lane = lax.broadcasted_iota(jnp.int32, (size, count), 1)
    by_key = [
        jnp.where(lane // (count // KVH) == k, q_lanes, jnp.zeros_like(q_lanes))
        for k in range(KVH)
    ]
    request = lax.broadcasted_iota(jnp.int32, (CTX, count), 1) % rows
    position = lax.broadcasted_iota(jnp.int32, (CTX, count), 0)
    spread = jnp.concatenate(by_key, axis=0)
    scores = jnp.zeros((CTX, count), F32)
    length = jnp.zeros((CTX, count), jnp.int32)
    for r in range(rows):
        k_copies[r].wait()
        all_lanes = jnp.dot(k_buf[r], spread, preferred_element_type=F32)
        scores = jnp.where(request == r, all_lanes, scores)
        length = jnp.where(request == r, len_ref[r], length)
    live = position < length
    scores = jnp.where(live, scores * (1.0 / math.sqrt(size)), -1e30)
    raw = jnp.where(live, jnp.exp(scores - jnp.max(scores, axis=0, keepdims=True)), 0.0)
    probs = (raw / jnp.sum(raw, axis=0, keepdims=True)).T.astype(BF16)
    owner = lax.broadcasted_iota(jnp.int32, (count, CTX), 0) % rows
    wide = jnp.zeros((count, KVH * size), F32)
    for r in range(rows):
        v_copies[r].wait()
        mine = jnp.where(owner == r, probs, jnp.zeros_like(probs))
        wide += jnp.dot(mine, v_buf[r], preferred_element_type=F32)
    group = count // KVH
    own = jnp.concatenate(
        [wide[k * group : (k + 1) * group, k * size : (k + 1) * size] for k in range(KVH)], axis=0
    ).astype(BF16)
    pair = 2 * rows
    for quad in range(QUERY_HEADS // QUAD):
        first = in_quad(quad, 0) * rows
        second = in_quad(quad, 2) * rows
        piece = jnp.concatenate([own[first : first + pair], own[second : second + pair]], axis=0)
        for m in range(QUAD):
            heads_ref[in_quad(quad, m)] = piece
    for copy in w_copies:
        copy.wait()


def start(member, lengths, queries, key_cache, value_cache, weight):
    rows = queries.shape[0]
    depth, columns = weight.shape
    piece = jax.ShapeDtypeStruct((depth, columns // QUAD), BF16)
    return pl.pallas_call(
        start_kernel,
        out_shape=(jax.ShapeDtypeStruct((QUERY_HEADS, QUAD * rows, HEAD_SIZE), BF16),)
        + (piece,) * (QUAD - 1),
        in_specs=[SMEM, SMEM, VMEM, HBM, HBM, HBM],
        out_specs=(VMEM,) + (HBM,) * (QUAD - 1),
        scratch_shapes=[
            pltpu.VMEM((rows, CTX, KVH * HEAD_SIZE), BF16),
            pltpu.VMEM((rows, CTX, KVH * HEAD_SIZE), BF16),
            pltpu.SemaphoreType.DMA((rows,)),
            pltpu.SemaphoreType.DMA((rows,)),
            pltpu.SemaphoreType.DMA((QUAD - 1, columns // QUAD // LINE)),
        ],
        compiler_params=pltpu.CompilerParams(vmem_limit_bytes=60 * 1024 * 1024),
        name="start",
    )(member, lengths, queries, key_cache, value_cache, weight)


def pick_rows(spans, index):
    count, size = spans.shape
    rows = count // QUAD
    row = lax.broadcasted_iota(jnp.int32, (rows, count), 0)
    column = lax.broadcasted_iota(jnp.int32, (rows, count), 1)
    wanted = (row // 4) * 16 + index * 4 + row % 4
    choice = jnp.where(column == wanted, 1.0, 0.0).astype(BF16)
    return jnp.dot(choice, spans, preferred_element_type=F32).astype(BF16)


def shrink_kernel(member_ref, block_ref, adapter_ref, spans_ref, down_ref, out_ref):
    devices, half, _ = out_ref.shape
    heads = pick_rows(spans_ref[...], member_ref[0])
    adapter = adapter_ref[...]
    rank = down_ref.shape[1]
    shrink = jnp.zeros((heads.shape[0], rank), F32)
    for b in range(down_ref.shape[0]):
        mine = jnp.where(adapter == block_ref[b], heads, jnp.zeros_like(heads))
        shrink += lax.dot_general(
            mine, down_ref[b], (((1,), (1,)), ((), ())), preferred_element_type=F32
        )
    for quad in range(devices // QUAD):
        base = quad * 2 * half
        pair = jnp.concatenate(
            [shrink[base : base + half], shrink[base + half : base + 2 * half]], axis=1
        ).astype(BF16)
        for m in range(QUAD):
            out_ref[in_quad(quad, m)] = pair


def shrink_parts(member, spans, down, adapter_col, block_adapter):
    devices = spans.shape[0] // (QUAD * 4)
    rows = spans.shape[0] // QUAD
    half = rows // (devices // QUAD) // 2
    return pl.pallas_call(
        shrink_kernel,
        out_shape=jax.ShapeDtypeStruct((devices, half, 2 * down.shape[2]), BF16),
        in_specs=[SMEM, SMEM, VMEM, VMEM, VMEM],
        out_specs=VMEM,
        compiler_params=PARAMS,
        name="shrink",
    )(member, block_adapter, adapter_col, spans, jnp.swapaxes(down, 1, 2))


def project_kernel(member_ref, spans_ref, *refs):
    weight_ref, *piece_refs, shrink_ref, out_ref = refs
    dests, _, width = out_ref.shape
    rows = spans_ref.shape[0] // QUAD
    spans = spans_ref[...]
    heads = jnp.concatenate(
        [pick_rows(spans, lax.bitwise_xor(member_ref[0], step)) for step in range(QUAD)],
        axis=1,
    )
    place = in_quad(0, member_ref[0])
    for d in range(dests):
        first = pl.multiple_of((in_quad(d, 0) + place) * width, width)
        columns = jnp.concatenate(
            [weight_ref[:, pl.ds(first, width)]]
            + [ref[:, d * width : (d + 1) * width] for ref in piece_refs],
            axis=0,
        )
        out_ref[d, :rows, :] = jnp.dot(heads, columns, preferred_element_type=F32).astype(BF16)
    low_rank = shrink_ref[0].astype(F32)
    for s in range(1, shrink_ref.shape[0]):
        low_rank += shrink_ref[s].astype(F32)
    wide = jnp.concatenate([low_rank, jnp.zeros_like(low_rank)], axis=1)
    block = jnp.concatenate([wide, jnp.zeros_like(wide)], axis=0).astype(BF16)
    for d in range(dests):
        out_ref[d, rows:, :] = block


def project(member, spans, weight, pieces, shrinks):
    rows = spans.shape[0] // QUAD
    dests = pieces[0].shape[1] // LINE
    return pl.pallas_call(
        project_kernel,
        out_shape=jax.ShapeDtypeStruct((dests, rows + 2 * shrinks.shape[1], LINE), BF16),
        in_specs=[SMEM] + [VMEM] * (QUAD + 2),
        out_specs=VMEM,
        compiler_params=PARAMS,
        name="project",
    )(member, spans, weight, *pieces, shrinks)


def finish_kernel(block_ref, adapter_ref, parts_ref, up_ref, out_ref):
    count = parts_ref.shape[0]
    rows, width = out_ref.shape
    blocks, rank, _ = up_ref.shape
    lanes = 2 * rank
    half = rows // count // 2
    left = lax.broadcasted_iota(jnp.int32, (half, lanes), 1) < rank
    pieces = []
    for s in range(count):
        pair = parts_ref[s, rows : rows + 2 * half, :lanes].astype(F32)[:half]
        turned = jnp.concatenate([pair[:, rank:], pair[:, :rank]], axis=1)
        pieces += [jnp.where(left, pair, turned), jnp.where(left, turned, pair)]
    low_rank = jnp.concatenate(pieces, axis=0)
    adapter = adapter_ref[...]
    wide_left = lax.broadcasted_iota(jnp.int32, (rows, lanes), 1) < rank
    spread = []
    for b in range(0, blocks, 2):
        match = jnp.where(wide_left, block_ref[b], block_ref[b + 1]) == adapter
        spread.append(jnp.where(match, low_rank, 0.0).astype(BF16))
    lora = jnp.dot(
        jnp.concatenate(spread, axis=1),
        up_ref[...].reshape(blocks * rank, width),
        preferred_element_type=F32,
    )
    total = parts_ref[0, :rows, :].astype(F32)
    for s in range(1, count):
        total += parts_ref[s, :rows, :].astype(F32)
    out_ref[...] = (total + lora).astype(BF16)


def finish(parts, up, adapter_col, block_adapter, rows):
    return pl.pallas_call(
        finish_kernel,
        out_shape=jax.ShapeDtypeStruct((rows, parts.shape[2]), BF16),
        in_specs=[SMEM, VMEM, VMEM, VMEM],
        out_specs=VMEM,
        compiler_params=PARAMS,
        name="finish",
    )(block_adapter, adapter_col, parts, up)


def per_device(
    devices,
    queries,
    key_cache,
    value_cache,
    lengths,
    request_adapter,
    block_adapter,
    output_weight,
    down_factors,
    up_factors,
):
    quads = devices // QUAD
    groups = [[in_quad(q, m) for q in range(quads)] for m in range(QUAD)]
    exchange = functools.partial(
        lax.all_to_all, axis_name="tp", split_axis=0, concat_axis=0, tiled=True
    )
    rows = request_adapter.shape[0]
    adapter_col = request_adapter[:, None]
    place = lax.axis_index("tp")
    member = ((place >> 2 & 1) * 2 + (place & 1)).astype(jnp.int32)[None]

    own, *weights = start(member, lengths, queries, key_cache, value_cache, output_weight)
    for step in range(1, QUAD):
        turn = [(in_quad(q, m), in_quad(q, m ^ step)) for q in range(quads) for m in range(QUAD)]
        weights[step - 1] = lax.ppermute(weights[step - 1], "tp", turn)
    spans = exchange(own).reshape(QUAD * rows, HEAD_SIZE)
    shrinks = exchange(shrink_parts(member, spans, down_factors, adapter_col, block_adapter))
    parts = exchange(project(member, spans, output_weight, weights, shrinks), axis_index_groups=groups)
    return finish(parts, up_factors, adapter_col, block_adapter, rows)


def solution(mesh):
    in_specs = (
        P(("rep", "tp"), None),
        P(("rep", "tp"), None, None),
        P(("rep", "tp"), None, None),
        P(("rep", "tp")),
        P("rep"),
        P("rep"),
        P("tp", None),
        P("rep", "tp", None),
        P("rep", None, "tp"),
    )
    return jax.shard_map(
        functools.partial(per_device, mesh.shape["tp"]),
        mesh=mesh,
        in_specs=in_specs,
        out_specs=P("rep", "tp"),
        check_vma=False,
    )
```

```python
import functools
import math

import jax
import jax.numpy as jnp
from jax import lax
from jax.experimental import pallas as pl
from jax.experimental.pallas import tpu as pltpu
from jax.sharding import PartitionSpec as P

HEAD_SIZE = 128
QUERY_HEADS = 32
KVH = 4
CTX = 256
QUAD = 4
LINE = 256
BF16, F32 = jnp.bfloat16, jnp.float32
VMEM = pl.BlockSpec(memory_space=pltpu.VMEM)
SMEM = pl.BlockSpec(memory_space=pltpu.SMEM)
HBM = pl.BlockSpec(memory_space=pltpu.HBM)
PARAMS = pltpu.CompilerParams(vmem_limit_bytes=16 * 1024 * 1024)
WHOLE = pltpu.CompilerParams(vmem_limit_bytes=60 * 1024 * 1024)


def in_quad(q, m):
    return q * QUAD + m


def regroup_kernel(steps, member_ref, w_hbm, *refs):
    *pieces, sem = refs
    copies = []
    for i, (step, piece) in enumerate(zip(steps, pieces)):
        m = lax.rem(member_ref[0] + step, QUAD)
        for q in range(piece.shape[1] // LINE):
            first = pl.multiple_of(in_quad(q, m) * LINE, LINE)
            copies.append(
                pltpu.make_async_copy(
                    w_hbm.at[:, pl.ds(first, LINE)], piece.at[:, pl.ds(q * LINE, LINE)], sem.at[i, q]
                )
            )
    for copy in copies:
        copy.start()
    for copy in copies:
        copy.wait()


def regroup(member, weight, steps):
    depth, columns = weight.shape
    piece = jax.ShapeDtypeStruct((depth, columns // QUAD), BF16)
    return pl.pallas_call(
        functools.partial(regroup_kernel, steps),
        out_shape=(piece,) * len(steps),
        in_specs=[SMEM, HBM],
        out_specs=(VMEM,) * len(steps),
        scratch_shapes=[pltpu.SemaphoreType.DMA((len(steps), columns // QUAD // LINE))],
        compiler_params=WHOLE,
        name="regroup",
    )(member, weight)


def attend_kernel(len_ref, q_ref, k_ref, v_ref, heads_ref):
    rows, size = k_ref.shape[0], HEAD_SIZE
    q = q_ref[...].astype(F32)
    q_rows = jnp.concatenate(
        [q[:, h * size : (h + 1) * size] for h in range(QUERY_HEADS)], axis=0
    )
    q_lanes = q_rows.T.astype(BF16)
    count = rows * QUERY_HEADS
    lane = lax.broadcasted_iota(jnp.int32, (size, count), 1)
    by_key = [
        jnp.where(lane // (count // KVH) == k, q_lanes, jnp.zeros_like(q_lanes))
        for k in range(KVH)
    ]
    request = lax.broadcasted_iota(jnp.int32, (CTX, count), 1) % rows
    position = lax.broadcasted_iota(jnp.int32, (CTX, count), 0)
    spread = jnp.concatenate(by_key, axis=0)
    scores = jnp.zeros((CTX, count), F32)
    length = jnp.zeros((CTX, count), jnp.int32)
    for r in range(rows):
        all_lanes = jnp.dot(k_ref[r], spread, preferred_element_type=F32)
        scores = jnp.where(request == r, all_lanes, scores)
        length = jnp.where(request == r, len_ref[r], length)
    live = position < length
    scores = jnp.where(live, scores * (1.0 / math.sqrt(size)), -1e30)
    raw = jnp.where(live, jnp.exp(scores - jnp.max(scores, axis=0, keepdims=True)), 0.0)
    probs = (raw / jnp.sum(raw, axis=0, keepdims=True)).T.astype(BF16)
    owner = lax.broadcasted_iota(jnp.int32, (count, CTX), 0) % rows
    wide = jnp.zeros((count, KVH * size), F32)
    for r in range(rows):
        mine = jnp.where(owner == r, probs, jnp.zeros_like(probs))
        wide += jnp.dot(mine, v_ref[r], preferred_element_type=F32)
    group = count // KVH
    own = jnp.concatenate(
        [wide[k * group : (k + 1) * group, k * size : (k + 1) * size] for k in range(KVH)], axis=0
    ).astype(BF16)
    span = QUAD * rows
    for quad in range(QUERY_HEADS // QUAD):
        for m in range(QUAD):
            heads_ref[in_quad(quad, m)] = own[quad * span : (quad + 1) * span]


def attend(lengths, queries, key_cache, value_cache):
    rows = queries.shape[0]
    return pl.pallas_call(
        attend_kernel,
        out_shape=jax.ShapeDtypeStruct((QUERY_HEADS, QUAD * rows, HEAD_SIZE), BF16),
        in_specs=[SMEM, VMEM, VMEM, VMEM],
        out_specs=VMEM,
        compiler_params=PARAMS,
        name="attend",
    )(lengths, queries, key_cache, value_cache)


def pick_rows(spans, index):
    count, size = spans.shape
    rows = count // QUAD
    row = lax.broadcasted_iota(jnp.int32, (rows, count), 0)
    column = lax.broadcasted_iota(jnp.int32, (rows, count), 1)
    wanted = (row // 4) * 16 + index * 4 + row % 4
    choice = jnp.where(column == wanted, 1.0, 0.0).astype(BF16)
    return jnp.dot(choice, spans, preferred_element_type=F32).astype(BF16)


def shrink_kernel(member_ref, block_ref, adapter_ref, spans_ref, down_ref, out_ref):
    half = out_ref.shape[1]
    heads = pick_rows(spans_ref[...], member_ref[0])
    adapter = adapter_ref[...]
    rank = down_ref.shape[1]
    shrink = jnp.zeros((heads.shape[0], rank), F32)
    for b in range(down_ref.shape[0]):
        mine = jnp.where(adapter == block_ref[b], heads, jnp.zeros_like(heads))
        shrink += lax.dot_general(
            mine, down_ref[b], (((1,), (1,)), ((), ())), preferred_element_type=F32
        )
    packed = jnp.concatenate([shrink[:half], shrink[half:]], axis=1).astype(BF16)
    for m in range(QUAD):
        out_ref[m] = packed


def shrink_parts(member, spans, down, adapter_col, block_adapter):
    half = spans.shape[0] // QUAD // 2
    return pl.pallas_call(
        shrink_kernel,
        out_shape=jax.ShapeDtypeStruct((QUAD, half, 2 * down.shape[2]), BF16),
        in_specs=[SMEM, SMEM, VMEM, VMEM, VMEM],
        out_specs=VMEM,
        compiler_params=PARAMS,
        name="shrink",
    )(member, block_adapter, adapter_col, spans, jnp.swapaxes(down, 1, 2))


def project_kernel(member_ref, spans_ref, *refs):
    weight_ref, *piece_refs, shrink_ref, out_ref = refs
    dests, _, width = out_ref.shape
    rows = spans_ref.shape[0] // QUAD
    spans = spans_ref[...]
    heads = jnp.concatenate(
        [pick_rows(spans, lax.rem(member_ref[0] + QUAD - step, QUAD)) for step in range(QUAD)],
        axis=1,
    )
    place = in_quad(0, member_ref[0])
    for d in range(dests):
        first = pl.multiple_of((in_quad(d, 0) + place) * width, width)
        columns = jnp.concatenate(
            [weight_ref[:, pl.ds(first, width)]]
            + [ref[:, d * width : (d + 1) * width] for ref in piece_refs],
            axis=0,
        )
        out_ref[d, :rows, :] = jnp.dot(heads, columns, preferred_element_type=F32).astype(BF16)
    shrink = shrink_ref[0].astype(F32)
    for m in range(1, QUAD):
        shrink += shrink_ref[m].astype(F32)
    half = shrink.shape[0] // 2
    packed = jnp.concatenate([shrink[:half], shrink[half:]], axis=1).astype(BF16)
    for d in range(dests):
        out_ref[d, rows:, :] = packed


def project(member, spans, weight, pieces, shrinks):
    rows = spans.shape[0] // QUAD
    dests = pieces[0].shape[1] // LINE
    return pl.pallas_call(
        project_kernel,
        out_shape=jax.ShapeDtypeStruct((dests, rows + shrinks.shape[1] // 2, LINE), BF16),
        in_specs=[SMEM] + [VMEM] * (QUAD + 2),
        out_specs=VMEM,
        compiler_params=PARAMS,
        name="project",
    )(member, spans, weight, *pieces, shrinks)


def finish_kernel(block_ref, adapter_ref, parts_ref, up_ref, out_ref):
    count = parts_ref.shape[0]
    rows, width = out_ref.shape
    blocks, rank, _ = up_ref.shape
    lanes = 2 * rank
    packed = parts_ref[0, rows:, :].astype(F32)
    for s in range(1, count):
        packed += parts_ref[s, rows:, :].astype(F32)
    pair = jnp.concatenate([packed[:, :lanes], packed[:, lanes:]], axis=0)
    turned = jnp.concatenate([pair[:, rank:], pair[:, :rank]], axis=1)
    left = lax.broadcasted_iota(jnp.int32, pair.shape, 1) < rank
    low_rank = jnp.concatenate(
        [jnp.where(left, pair, turned), jnp.where(left, turned, pair)], axis=0
    )
    adapter = adapter_ref[...]
    wide_left = lax.broadcasted_iota(jnp.int32, (rows, lanes), 1) < rank
    spread = []
    for b in range(0, blocks, 2):
        match = jnp.where(wide_left, block_ref[b], block_ref[b + 1]) == adapter
        spread.append(jnp.where(match, low_rank, 0.0).astype(BF16))
    lora = jnp.dot(
        jnp.concatenate(spread, axis=1),
        up_ref[...].reshape(blocks * rank, width),
        preferred_element_type=F32,
    )
    total = parts_ref[0, :rows, :].astype(F32)
    for s in range(1, count):
        total += parts_ref[s, :rows, :].astype(F32)
    out_ref[...] = (total + lora).astype(BF16)


def finish(parts, up, adapter_col, block_adapter, rows):
    return pl.pallas_call(
        finish_kernel,
        out_shape=jax.ShapeDtypeStruct((rows, parts.shape[2]), BF16),
        in_specs=[SMEM, VMEM, VMEM, VMEM],
        out_specs=VMEM,
        compiler_params=PARAMS,
        name="finish",
    )(block_adapter, adapter_col, parts, up)


def per_device(
    devices,
    queries,
    key_cache,
    value_cache,
    lengths,
    request_adapter,
    block_adapter,
    output_weight,
    down_factors,
    up_factors,
):
    quads = devices // QUAD
    groups = [[in_quad(q, m) for q in range(quads)] for m in range(QUAD)]
    lines = [[in_quad(q, m) for m in range(QUAD)] for q in range(quads)]
    exchange = functools.partial(
        lax.all_to_all, axis_name="tp", split_axis=0, concat_axis=0, tiled=True
    )
    rows = request_adapter.shape[0]
    adapter_col = request_adapter[:, None]
    member = (lax.axis_index("tp") & (QUAD - 1)).astype(jnp.int32)[None]

    def ahead(piece, step):
        turn = [
            (in_quad(q, m), in_quad(q, (m + step) % QUAD)) for q in range(quads) for m in range(QUAD)
        ]
        return lax.ppermute(piece, "tp", turn)

    steps = range(1, QUAD)
    weights = regroup(member, output_weight, steps)
    weights = [ahead(piece, step) for piece, step in zip(weights, steps)]
    own = attend(lengths, queries, key_cache, value_cache)
    spans = exchange(own).reshape(QUAD * rows, HEAD_SIZE)
    shrinks = exchange(
        shrink_parts(member, spans, down_factors, adapter_col, block_adapter),
        axis_index_groups=lines,
    )
    parts = exchange(project(member, spans, output_weight, weights, shrinks), axis_index_groups=groups)
    return finish(parts, up_factors, adapter_col, block_adapter, rows)


def solution(mesh):
    in_specs = (
        P(("rep", "tp"), None),
        P(("rep", "tp"), None, None),
        P(("rep", "tp"), None, None),
        P(("rep", "tp")),
        P("rep"),
        P("rep"),
        P("tp", None),
        P("rep", "tp", None),
        P("rep", None, "tp"),
    )
    return jax.shard_map(
        functools.partial(per_device, mesh.shape["tp"]),
        mesh=mesh,
        in_specs=in_specs,
        out_specs=P("rep", "tp"),
        check_vma=False,
    )
```

```python
import functools
import math

import jax
import jax.numpy as jnp
from jax import lax
from jax.experimental import pallas as pl
from jax.experimental.pallas import tpu as pltpu
from jax.sharding import PartitionSpec as P

HEAD_SIZE = 128
QUERY_HEADS = 32
KVH = 4
CTX = 256
QUAD = 4
LINE = 256
BF16, F32 = jnp.bfloat16, jnp.float32
VMEM = pl.BlockSpec(memory_space=pltpu.VMEM)
SMEM = pl.BlockSpec(memory_space=pltpu.SMEM)
HBM = pl.BlockSpec(memory_space=pltpu.HBM)
PARAMS = pltpu.CompilerParams(vmem_limit_bytes=16 * 1024 * 1024)
WHOLE = pltpu.CompilerParams(vmem_limit_bytes=60 * 1024 * 1024)


def in_quad(q, m):
    return q * QUAD + m


def start_kernel(
    place_ref, len_ref, q_ref, k_hbm, v_hbm, w_hbm, heads_ref, near_ref, far_ref, k_ref, v_ref, k_sem, v_sem, w_sem
):
    rows, size = k_ref.shape[0], HEAD_SIZE
    k_copies = [pltpu.make_async_copy(k_hbm.at[r], k_ref.at[r], k_sem.at[r]) for r in range(rows)]
    v_copies = [pltpu.make_async_copy(v_hbm.at[r], v_ref.at[r], v_sem.at[r]) for r in range(rows)]
    member, core = place_ref[0] & (QUAD - 1), lax.div(place_ref[0], QUAD)
    near = lax.rem(member + 1 + 2 * core, QUAD)
    far = lax.rem(member + 2, QUAD)
    depth = far_ref.shape[0]
    half = pl.ds(pl.multiple_of(core * depth, depth), depth)
    w_copies = []
    for q in range(near_ref.shape[1] // LINE):
        columns = pl.ds(q * LINE, LINE)
        source = pl.ds(pl.multiple_of(in_quad(q, near) * LINE, LINE), LINE)
        w_copies.append(
            pltpu.make_async_copy(w_hbm.at[:, source], near_ref.at[:, columns], w_sem.at[0, q])
        )
        source = pl.ds(pl.multiple_of(in_quad(q, far) * LINE, LINE), LINE)
        w_copies.append(
            pltpu.make_async_copy(w_hbm.at[half, source], far_ref.at[:, columns], w_sem.at[1, q])
        )
    for copy in k_copies + v_copies + w_copies:
        copy.start()

    q = q_ref[...].astype(F32)
    q_rows = jnp.concatenate(
        [q[:, h * size : (h + 1) * size] for h in range(QUERY_HEADS)], axis=0
    )
    q_lanes = q_rows.T.astype(BF16)
    count = rows * QUERY_HEADS
    lane = lax.broadcasted_iota(jnp.int32, (size, count), 1)
    by_key = [
        jnp.where(lane // (count // KVH) == k, q_lanes, jnp.zeros_like(q_lanes))
        for k in range(KVH)
    ]
    request = lax.broadcasted_iota(jnp.int32, (CTX, count), 1) % rows
    position = lax.broadcasted_iota(jnp.int32, (CTX, count), 0)
    spread = jnp.concatenate(by_key, axis=0)
    scores = jnp.zeros((CTX, count), F32)
    length = jnp.zeros((CTX, count), jnp.int32)
    for r in range(rows):
        k_copies[r].wait()
        all_lanes = jnp.dot(k_ref[r], spread, preferred_element_type=F32)
        scores = jnp.where(request == r, all_lanes, scores)
        length = jnp.where(request == r, len_ref[r], length)
    live = position < length
    scores = jnp.where(live, scores * (1.0 / math.sqrt(size)), -1e30)
    raw = jnp.where(live, jnp.exp(scores - jnp.max(scores, axis=0, keepdims=True)), 0.0)
    probs = (raw / jnp.sum(raw, axis=0, keepdims=True)).T.astype(BF16)
    owner = lax.broadcasted_iota(jnp.int32, (count, CTX), 0) % rows
    wide = jnp.zeros((count, KVH * size), F32)
    for r in range(rows):
        v_copies[r].wait()
        mine = jnp.where(owner == r, probs, jnp.zeros_like(probs))
        wide += jnp.dot(mine, v_ref[r], preferred_element_type=F32)
    group = count // KVH
    own = jnp.concatenate(
        [wide[k * group : (k + 1) * group, k * size : (k + 1) * size] for k in range(KVH)], axis=0
    ).astype(BF16)
    span = QUAD * rows
    for quad in range(QUERY_HEADS // QUAD):
        for m in range(QUAD):
            heads_ref[in_quad(quad, m)] = own[quad * span : (quad + 1) * span]
    for copy in w_copies:
        copy.wait()


def start(place, lengths, queries, key_cache, value_cache, weight):
    rows = queries.shape[0]
    depth, columns = weight.shape
    span = columns // QUAD
    cache = pltpu.VMEM((rows, CTX, KVH * HEAD_SIZE), BF16)
    return pl.pallas_call(
        start_kernel,
        out_shape=(
            jax.ShapeDtypeStruct((QUERY_HEADS, QUAD * rows, HEAD_SIZE), BF16),
            jax.ShapeDtypeStruct((depth, span), BF16),
            jax.ShapeDtypeStruct((depth // 2, span), BF16),
        ),
        in_specs=[SMEM, SMEM, VMEM, HBM, HBM, HBM],
        out_specs=(VMEM,) * 3,
        scratch_shapes=[cache, cache]
        + [pltpu.SemaphoreType.DMA((rows,))] * 2
        + [pltpu.SemaphoreType.DMA((2, span // LINE))],
        compiler_params=WHOLE,
        name="start",
    )(place, lengths, queries, key_cache, value_cache, weight)


def pick_rows(spans, index):
    count, size = spans.shape
    rows = count // QUAD
    row = lax.broadcasted_iota(jnp.int32, (rows, count), 0)
    column = lax.broadcasted_iota(jnp.int32, (rows, count), 1)
    wanted = (row // 4) * 16 + index * 4 + row % 4
    choice = jnp.where(column == wanted, 1.0, 0.0).astype(BF16)
    return jnp.dot(choice, spans, preferred_element_type=F32).astype(BF16)


def shrink_kernel(place_ref, block_ref, adapter_ref, spans_ref, down_ref, out_ref):
    half = out_ref.shape[1]
    heads = pick_rows(spans_ref[...], place_ref[0] & (QUAD - 1))
    adapter = adapter_ref[...]
    rank = down_ref.shape[1]
    shrink = jnp.zeros((heads.shape[0], rank), F32)
    for b in range(down_ref.shape[0]):
        mine = jnp.where(adapter == block_ref[b], heads, jnp.zeros_like(heads))
        shrink += lax.dot_general(
            mine, down_ref[b], (((1,), (1,)), ((), ())), preferred_element_type=F32
        )
    packed = jnp.concatenate([shrink[:half], shrink[half:]], axis=1).astype(BF16)
    for m in range(QUAD):
        out_ref[m] = packed


def shrink_parts(place, spans, down, adapter_col, block_adapter):
    half = spans.shape[0] // QUAD // 2
    return pl.pallas_call(
        shrink_kernel,
        out_shape=jax.ShapeDtypeStruct((QUAD, half, 2 * down.shape[2]), BF16),
        in_specs=[SMEM, SMEM, VMEM, VMEM, VMEM],
        out_specs=VMEM,
        compiler_params=PARAMS,
        name="shrink",
    )(place, block_adapter, adapter_col, spans, jnp.swapaxes(down, 1, 2))


def arrange_kernel(place_ref, spans_ref, out_ref):
    spans = spans_ref[...]
    member, core = place_ref[0] & (QUAD - 1), lax.div(place_ref[0], QUAD)
    near, other = lax.rem(member + 3 + 2 * core, QUAD), lax.rem(member + 1 + 2 * core, QUAD)
    size = spans.shape[1]
    for i, block in enumerate((member, near, other)):
        out_ref[:, i * size : (i + 1) * size] = pick_rows(spans, block)
    opposite = pick_rows(spans, lax.rem(member + 2, QUAD))
    turned = jnp.concatenate([opposite[:, size // 2 :], opposite[:, : size // 2]], axis=1)
    out_ref[:, 3 * size :] = jnp.where(core == 0, opposite, turned)


def arrange(place, spans):
    count, size = spans.shape
    return pl.pallas_call(
        arrange_kernel,
        out_shape=jax.ShapeDtypeStruct((count // QUAD, QUAD * size), BF16),
        in_specs=[SMEM, VMEM],
        out_specs=VMEM,
        compiler_params=PARAMS,
        cost_estimate=pl.CostEstimate(flops=2 * 10**10, bytes_accessed=2**18, transcendentals=0),
        name="arrange",
    )(place, spans)


def project_kernel(
    place_ref, heads_ref, weight_ref, near_ref, far_ref, other_ref, shrink_ref, out_ref
):
    dests, _, width = out_ref.shape
    rows = heads_ref.shape[0]
    heads = heads_ref[...]
    member, depth = place_ref[0] & (QUAD - 1), far_ref.shape[0]
    for d in range(dests):
        first = pl.multiple_of(in_quad(d, member) * width, width)
        columns = pl.ds(d * width, width)
        stacked = jnp.concatenate(
            [
                weight_ref[:, pl.ds(first, width)],
                near_ref[:, columns],
                other_ref[: 2 * depth, columns],
                far_ref[:, columns],
                other_ref[2 * depth :, columns],
            ],
            axis=0,
        )
        out_ref[d, :rows, :] = jnp.dot(heads, stacked, preferred_element_type=F32).astype(BF16)
    shrink = shrink_ref[0].astype(F32)
    for m in range(1, QUAD):
        shrink += shrink_ref[m].astype(F32)
    half = shrink.shape[0] // 2
    packed = jnp.concatenate([shrink[:half], shrink[half:]], axis=1).astype(BF16)
    for d in range(dests):
        out_ref[d, rows:, :] = packed


def project(place, heads, weight, near, far, other, shrinks):
    rows = heads.shape[0]
    dests = near.shape[1] // LINE
    return pl.pallas_call(
        project_kernel,
        out_shape=jax.ShapeDtypeStruct((dests, rows + shrinks.shape[1] // 2, LINE), BF16),
        in_specs=[SMEM] + [VMEM] * 6,
        out_specs=VMEM,
        compiler_params=PARAMS,
        name="project",
    )(place, heads, weight, near, far, other, shrinks)


def finish_kernel(block_ref, adapter_ref, parts_ref, up_ref, out_ref):
    count = parts_ref.shape[0]
    rows, width = out_ref.shape
    blocks, rank, _ = up_ref.shape
    lanes = 2 * rank
    packed = parts_ref[0, rows:, :].astype(F32)
    for s in range(1, count):
        packed += parts_ref[s, rows:, :].astype(F32)
    pair = jnp.concatenate([packed[:, :lanes], packed[:, lanes:]], axis=0)
    turned = jnp.concatenate([pair[:, rank:], pair[:, :rank]], axis=1)
    left = lax.broadcasted_iota(jnp.int32, pair.shape, 1) < rank
    low_rank = jnp.concatenate(
        [jnp.where(left, pair, turned), jnp.where(left, turned, pair)], axis=0
    )
    adapter = adapter_ref[...]
    wide_left = lax.broadcasted_iota(jnp.int32, (rows, lanes), 1) < rank
    spread = []
    for b in range(0, blocks, 2):
        match = jnp.where(wide_left, block_ref[b], block_ref[b + 1]) == adapter
        spread.append(jnp.where(match, low_rank, 0.0).astype(BF16))
    lora = jnp.dot(
        jnp.concatenate(spread, axis=1),
        up_ref[...].reshape(blocks * rank, width),
        preferred_element_type=F32,
    )
    total = parts_ref[0, :rows, :].astype(F32)
    for s in range(1, count):
        total += parts_ref[s, :rows, :].astype(F32)
    out_ref[...] = (total + lora).astype(BF16)


def finish(parts, up, adapter_col, block_adapter, rows):
    return pl.pallas_call(
        finish_kernel,
        out_shape=jax.ShapeDtypeStruct((rows, parts.shape[2]), BF16),
        in_specs=[SMEM, VMEM, VMEM, VMEM],
        out_specs=VMEM,
        compiler_params=PARAMS,
        name="finish",
    )(block_adapter, adapter_col, parts, up)


def per_device(
    reps,
    devices,
    queries,
    key_cache,
    value_cache,
    lengths,
    request_adapter,
    block_adapter,
    output_weight,
    down_factors,
    up_factors,
):
    quads = devices // QUAD
    groups = [[in_quad(q, m) for q in range(quads)] for m in range(QUAD)]
    lines = [[in_quad(q, m) for m in range(QUAD)] for q in range(quads)]
    exchange = functools.partial(
        lax.all_to_all, axis_name="tp", split_axis=0, concat_axis=0, tiled=True
    )
    rows = request_adapter.shape[0]
    adapter_col = request_adapter[:, None]
    place = (lax.axis_index("tp") & (QUAD - 1)) + (lax.axis_index("rep") & 1) * QUAD
    place = place.astype(jnp.int32)[None]

    own, near, far = start(place, lengths, queries, key_cache, value_cache, output_weight)
    near = lax.ppermute(
        near,
        ("rep", "tp"),
        [
            (r * devices + in_quad(q, m), r * devices + in_quad(q, (m + 1 + 2 * (r & 1)) % QUAD))
            for r in range(reps)
            for q in range(quads)
            for m in range(QUAD)
        ],
    )
    far = lax.ppermute(
        far, "tp", [(in_quad(q, m), in_quad(q, (m + 2) % QUAD)) for q in range(quads) for m in range(QUAD)]
    )
    spans = exchange(own).reshape(QUAD * rows, HEAD_SIZE)
    partial = shrink_parts(place, spans, down_factors, adapter_col, block_adapter)
    shrinks = exchange(partial, axis_index_groups=lines)
    held, _ = lax.optimization_barrier((jnp.concatenate([near, far], axis=0), partial))
    other = lax.ppermute(held, "rep", [(r, r ^ 1) for r in range(reps)])
    heads = arrange(place, spans)
    parts = exchange(
        project(place, heads, output_weight, near, far, other, shrinks), axis_index_groups=groups
    )
    return finish(parts, up_factors, adapter_col, block_adapter, rows)


def solution(mesh):
    in_specs = (
        P(("rep", "tp"), None),
        P(("rep", "tp"), None, None),
        P(("rep", "tp"), None, None),
        P(("rep", "tp")),
        P("rep"),
        P("rep"),
        P("tp", None),
        P("rep", "tp", None),
        P("rep", None, "tp"),
    )
    return jax.shard_map(
        functools.partial(per_device, mesh.shape["rep"], mesh.shape["tp"]),
        mesh=mesh,
        in_specs=in_specs,
        out_specs=P("rep", "tp"),
        check_vma=False,
    )
```

```python
import functools
import math

import jax
import jax.numpy as jnp
from jax import lax
from jax.experimental import pallas as pl
from jax.experimental.pallas import tpu as pltpu
from jax.sharding import PartitionSpec as P

HEAD_SIZE = 128
QUERY_HEADS = 32
KVH = 4
CTX = 256
QUAD = 4
LINE = 256
BF16, F32 = jnp.bfloat16, jnp.float32
VMEM = pl.BlockSpec(memory_space=pltpu.VMEM)
SMEM = pl.BlockSpec(memory_space=pltpu.SMEM)
HBM = pl.BlockSpec(memory_space=pltpu.HBM)
PARAMS = pltpu.CompilerParams(vmem_limit_bytes=16 * 1024 * 1024)
WHOLE = pltpu.CompilerParams(vmem_limit_bytes=60 * 1024 * 1024)


def in_quad(q, m):
    return q * QUAD + m


def start_kernel(
    place_ref, len_ref, q_ref, k_hbm, v_hbm, w_hbm, heads_ref, near_ref, far_ref, k_ref, v_ref, k_sem, v_sem, w_sem
):
    rows, size = k_ref.shape[0], HEAD_SIZE
    k_copies = [pltpu.make_async_copy(k_hbm.at[r], k_ref.at[r], k_sem.at[r]) for r in range(rows)]
    v_copies = [pltpu.make_async_copy(v_hbm.at[r], v_ref.at[r], v_sem.at[r]) for r in range(rows)]
    member, core = place_ref[0] & (QUAD - 1), lax.div(place_ref[0], QUAD)
    near = lax.rem(member + 1 + 2 * core, QUAD)
    far = lax.rem(member + 2, QUAD)
    depth = far_ref.shape[0]
    half = pl.ds(pl.multiple_of(core * depth, depth), depth)
    w_copies = []
    for q in range(near_ref.shape[1] // LINE):
        columns = pl.ds(q * LINE, LINE)
        source = pl.ds(pl.multiple_of(in_quad(q, near) * LINE, LINE), LINE)
        w_copies.append(
            pltpu.make_async_copy(w_hbm.at[:, source], near_ref.at[:, columns], w_sem.at[0, q])
        )
        source = pl.ds(pl.multiple_of(in_quad(q, far) * LINE, LINE), LINE)
        w_copies.append(
            pltpu.make_async_copy(w_hbm.at[half, source], far_ref.at[:, columns], w_sem.at[1, q])
        )
    for copy in k_copies + v_copies + w_copies:
        copy.start()

    q = q_ref[...].astype(F32)
    q_rows = jnp.concatenate(
        [q[:, h * size : (h + 1) * size] for h in range(QUERY_HEADS)], axis=0
    )
    q_lanes = q_rows.T.astype(BF16)
    count = rows * QUERY_HEADS
    lane = lax.broadcasted_iota(jnp.int32, (size, count), 1)
    by_key = [
        jnp.where(lane // (count // KVH) == k, q_lanes, jnp.zeros_like(q_lanes))
        for k in range(KVH)
    ]
    request = lax.broadcasted_iota(jnp.int32, (CTX, count), 1) % rows
    position = lax.broadcasted_iota(jnp.int32, (CTX, count), 0)
    spread = jnp.concatenate(by_key, axis=0)
    scores = jnp.zeros((CTX, count), F32)
    length = jnp.zeros((CTX, count), jnp.int32)
    for r in range(rows):
        k_copies[r].wait()
        all_lanes = jnp.dot(k_ref[r], spread, preferred_element_type=F32)
        scores = jnp.where(request == r, all_lanes, scores)
        length = jnp.where(request == r, len_ref[r], length)
    live = position < length
    scores = jnp.where(live, scores * (1.0 / math.sqrt(size)), -1e30)
    raw = jnp.where(live, jnp.exp(scores - jnp.max(scores, axis=0, keepdims=True)), 0.0)
    probs = (raw / jnp.sum(raw, axis=0, keepdims=True)).T.astype(BF16)
    owner = lax.broadcasted_iota(jnp.int32, (count, CTX), 0) % rows
    wide = jnp.zeros((count, KVH * size), F32)
    for r in range(rows):
        v_copies[r].wait()
        mine = jnp.where(owner == r, probs, jnp.zeros_like(probs))
        wide += jnp.dot(mine, v_ref[r], preferred_element_type=F32)
    group = count // KVH
    own = jnp.concatenate(
        [wide[k * group : (k + 1) * group, k * size : (k + 1) * size] for k in range(KVH)], axis=0
    ).astype(BF16)
    span = QUAD * rows
    for quad in range(QUERY_HEADS // QUAD):
        for m in range(QUAD):
            heads_ref[in_quad(quad, m)] = own[quad * span : (quad + 1) * span]
    for copy in w_copies:
        copy.wait()


def start(place, lengths, queries, key_cache, value_cache, weight):
    rows = queries.shape[0]
    depth, columns = weight.shape
    span = columns // QUAD
    cache = pltpu.VMEM((rows, CTX, KVH * HEAD_SIZE), BF16)
    return pl.pallas_call(
        start_kernel,
        out_shape=(
            jax.ShapeDtypeStruct((QUERY_HEADS, QUAD * rows, HEAD_SIZE), BF16),
            jax.ShapeDtypeStruct((depth, span), BF16),
            jax.ShapeDtypeStruct((depth // 2, span), BF16),
        ),
        in_specs=[SMEM, SMEM, VMEM, HBM, HBM, HBM],
        out_specs=(VMEM,) * 3,
        scratch_shapes=[cache, cache]
        + [pltpu.SemaphoreType.DMA((rows,))] * 2
        + [pltpu.SemaphoreType.DMA((2, span // LINE))],
        compiler_params=WHOLE,
        name="start",
    )(place, lengths, queries, key_cache, value_cache, weight)


def pick_rows(spans, index):
    count, size = spans.shape
    rows = count // QUAD
    row = lax.broadcasted_iota(jnp.int32, (rows, count), 0)
    column = lax.broadcasted_iota(jnp.int32, (rows, count), 1)
    wanted = (row // 4) * 16 + index * 4 + row % 4
    choice = jnp.where(column == wanted, 1.0, 0.0).astype(BF16)
    return jnp.dot(choice, spans, preferred_element_type=F32).astype(BF16)


def shrink_kernel(place_ref, block_ref, adapter_ref, spans_ref, down_ref, out_ref):
    half = out_ref.shape[1]
    heads = pick_rows(spans_ref[...], place_ref[0] & (QUAD - 1))
    adapter = adapter_ref[...]
    rank = down_ref.shape[1]
    shrink = jnp.zeros((heads.shape[0], rank), F32)
    for b in range(down_ref.shape[0]):
        mine = jnp.where(adapter == block_ref[b], heads, jnp.zeros_like(heads))
        shrink += lax.dot_general(
            mine, down_ref[b], (((1,), (1,)), ((), ())), preferred_element_type=F32
        )
    packed = jnp.concatenate([shrink[:half], shrink[half:]], axis=1).astype(BF16)
    for m in range(QUAD):
        out_ref[m] = packed


def shrink_parts(place, spans, down, adapter_col, block_adapter):
    half = spans.shape[0] // QUAD // 2
    return pl.pallas_call(
        shrink_kernel,
        out_shape=jax.ShapeDtypeStruct((QUAD, half, 2 * down.shape[2]), BF16),
        in_specs=[SMEM, SMEM, VMEM, VMEM, VMEM],
        out_specs=VMEM,
        compiler_params=PARAMS,
        cost_estimate=pl.CostEstimate(flops=10**9, bytes_accessed=2**20, transcendentals=0),
        name="shrink",
    )(place, block_adapter, adapter_col, spans, jnp.swapaxes(down, 1, 2))


def arrange_kernel(place_ref, spans_ref, out_ref):
    spans = spans_ref[...]
    member, core = place_ref[0] & (QUAD - 1), lax.div(place_ref[0], QUAD)
    near, other = lax.rem(member + 3 + 2 * core, QUAD), lax.rem(member + 1 + 2 * core, QUAD)
    size = spans.shape[1]
    for i, block in enumerate((member, near, other)):
        out_ref[:, i * size : (i + 1) * size] = pick_rows(spans, block)
    opposite = pick_rows(spans, lax.rem(member + 2, QUAD))
    turned = jnp.concatenate([opposite[:, size // 2 :], opposite[:, : size // 2]], axis=1)
    out_ref[:, 3 * size :] = jnp.where(core == 0, opposite, turned)


def arrange(place, spans):
    count, size = spans.shape
    return pl.pallas_call(
        arrange_kernel,
        out_shape=jax.ShapeDtypeStruct((count // QUAD, QUAD * size), BF16),
        in_specs=[SMEM, VMEM],
        out_specs=VMEM,
        compiler_params=PARAMS,
        cost_estimate=pl.CostEstimate(flops=2 * 10**10, bytes_accessed=2**18, transcendentals=0),
        name="arrange",
    )(place, spans)


def project_kernel(
    place_ref, heads_ref, weight_ref, near_ref, far_ref, other_ref, shrink_ref, out_ref
):
    dests, _, width = out_ref.shape
    rows = heads_ref.shape[0]
    heads = heads_ref[...]
    member, depth = place_ref[0] & (QUAD - 1), far_ref.shape[0]
    for d in range(dests):
        first = pl.multiple_of(in_quad(d, member) * width, width)
        columns = pl.ds(d * width, width)
        stacked = jnp.concatenate(
            [
                weight_ref[:, pl.ds(first, width)],
                near_ref[:, columns],
                other_ref[: 2 * depth, columns],
                far_ref[:, columns],
                other_ref[2 * depth :, columns],
            ],
            axis=0,
        )
        out_ref[d, :rows, :] = jnp.dot(heads, stacked, preferred_element_type=F32).astype(BF16)
    shrink = shrink_ref[0].astype(F32)
    for m in range(1, QUAD):
        shrink += shrink_ref[m].astype(F32)
    half = shrink.shape[0] // 2
    packed = jnp.concatenate([shrink[:half], shrink[half:]], axis=1).astype(BF16)
    for d in range(dests):
        out_ref[d, rows:, :] = packed


def project(place, heads, weight, near, far, other, shrinks):
    rows = heads.shape[0]
    dests = near.shape[1] // LINE
    return pl.pallas_call(
        project_kernel,
        out_shape=jax.ShapeDtypeStruct((dests, rows + shrinks.shape[1] // 2, LINE), BF16),
        in_specs=[SMEM] + [VMEM] * 6,
        out_specs=VMEM,
        compiler_params=PARAMS,
        name="project",
    )(place, heads, weight, near, far, other, shrinks)


def finish_kernel(block_ref, adapter_ref, parts_ref, up_ref, out_ref):
    count = parts_ref.shape[0]
    rows, width = out_ref.shape
    blocks, rank, _ = up_ref.shape
    lanes = 2 * rank
    packed = parts_ref[0, rows:, :].astype(F32)
    for s in range(1, count):
        packed += parts_ref[s, rows:, :].astype(F32)
    pair = jnp.concatenate([packed[:, :lanes], packed[:, lanes:]], axis=0)
    turned = jnp.concatenate([pair[:, rank:], pair[:, :rank]], axis=1)
    left = lax.broadcasted_iota(jnp.int32, pair.shape, 1) < rank
    low_rank = jnp.concatenate(
        [jnp.where(left, pair, turned), jnp.where(left, turned, pair)], axis=0
    )
    adapter = adapter_ref[...]
    wide_left = lax.broadcasted_iota(jnp.int32, (rows, lanes), 1) < rank
    spread = []
    for b in range(0, blocks, 2):
        match = jnp.where(wide_left, block_ref[b], block_ref[b + 1]) == adapter
        spread.append(jnp.where(match, low_rank, 0.0).astype(BF16))
    lora = jnp.dot(
        jnp.concatenate(spread, axis=1),
        up_ref[...].reshape(blocks * rank, width),
        preferred_element_type=F32,
    )
    total = parts_ref[0, :rows, :].astype(F32)
    for s in range(1, count):
        total += parts_ref[s, :rows, :].astype(F32)
    out_ref[...] = (total + lora).astype(BF16)


def finish(parts, up, adapter_col, block_adapter, rows):
    return pl.pallas_call(
        finish_kernel,
        out_shape=jax.ShapeDtypeStruct((rows, parts.shape[2]), BF16),
        in_specs=[SMEM, VMEM, VMEM, VMEM],
        out_specs=VMEM,
        compiler_params=PARAMS,
        name="finish",
    )(block_adapter, adapter_col, parts, up)


def per_device(
    reps,
    devices,
    queries,
    key_cache,
    value_cache,
    lengths,
    request_adapter,
    block_adapter,
    output_weight,
    down_factors,
    up_factors,
):
    quads = devices // QUAD
    groups = [[in_quad(q, m) for q in range(quads)] for m in range(QUAD)]
    lines = [[in_quad(q, m) for m in range(QUAD)] for q in range(quads)]
    exchange = functools.partial(
        lax.all_to_all, axis_name="tp", split_axis=0, concat_axis=0, tiled=True
    )
    rows = request_adapter.shape[0]
    adapter_col = request_adapter[:, None]
    place = (lax.axis_index("tp") & (QUAD - 1)) + (lax.axis_index("rep") & 1) * QUAD
    place = place.astype(jnp.int32)[None]

    own, near, far = start(place, lengths, queries, key_cache, value_cache, output_weight)
    near = lax.ppermute(
        near,
        ("rep", "tp"),
        [
            (r * devices + in_quad(q, m), r * devices + in_quad(q, (m + 1 + 2 * (r & 1)) % QUAD))
            for r in range(reps)
            for q in range(quads)
            for m in range(QUAD)
        ],
    )
    far = lax.ppermute(
        far, "tp", [(in_quad(q, m), in_quad(q, (m + 2) % QUAD)) for q in range(quads) for m in range(QUAD)]
    )
    spans = exchange(own).reshape(QUAD * rows, HEAD_SIZE)
    partial = shrink_parts(place, spans, down_factors, adapter_col, block_adapter)
    shrinks = exchange(partial, axis_index_groups=lines)
    held, _ = lax.optimization_barrier((jnp.concatenate([near, far], axis=0), partial))
    other = lax.ppermute(held, "rep", [(r, r ^ 1) for r in range(reps)])
    heads = arrange(place, spans)
    parts = exchange(
        project(place, heads, output_weight, near, far, other, shrinks), axis_index_groups=groups
    )
    return finish(parts, up_factors, adapter_col, block_adapter, rows)


def solution(mesh):
    in_specs = (
        P(("rep", "tp"), None),
        P(("rep", "tp"), None, None),
        P(("rep", "tp"), None, None),
        P(("rep", "tp")),
        P("rep"),
        P("rep"),
        P("tp", None),
        P("rep", "tp", None),
        P("rep", None, "tp"),
    )
    return jax.shard_map(
        functools.partial(per_device, mesh.shape["rep"], mesh.shape["tp"]),
        mesh=mesh,
        in_specs=in_specs,
        out_specs=P("rep", "tp"),
        check_vma=False,
    )
```

```python
import functools
import math

import jax
import jax.numpy as jnp
from jax import lax
from jax.experimental import pallas as pl
from jax.experimental.pallas import tpu as pltpu
from jax.sharding import PartitionSpec as P

HEAD_SIZE = 128
QUERY_HEADS = 32
KVH = 4
CTX = 256
QUAD = 4
LINE = 256
BF16, F32 = jnp.bfloat16, jnp.float32
VMEM = pl.BlockSpec(memory_space=pltpu.VMEM)
SMEM = pl.BlockSpec(memory_space=pltpu.SMEM)
HBM = pl.BlockSpec(memory_space=pltpu.HBM)
PARAMS = pltpu.CompilerParams(vmem_limit_bytes=16 * 1024 * 1024)
WHOLE = pltpu.CompilerParams(vmem_limit_bytes=60 * 1024 * 1024)


def in_quad(q, m):
    return q * QUAD + m


def start_kernel(
    place_ref, len_ref, q_ref, k_hbm, v_hbm, w_hbm, heads_ref, near_ref, far_ref, k_ref, v_ref, k_sem, v_sem, w_sem
):
    rows, size = k_ref.shape[0], HEAD_SIZE
    k_copies = [pltpu.make_async_copy(k_hbm.at[r], k_ref.at[r], k_sem.at[r]) for r in range(rows)]
    v_copies = [pltpu.make_async_copy(v_hbm.at[r], v_ref.at[r], v_sem.at[r]) for r in range(rows)]
    member, core = place_ref[0] & (QUAD - 1), lax.div(place_ref[0], QUAD)
    near = lax.rem(member + 1 + 2 * core, QUAD)
    far = lax.rem(member + 2, QUAD)
    depth = far_ref.shape[0]
    half = pl.ds(pl.multiple_of(core * depth, depth), depth)
    w_copies = []
    for q in range(near_ref.shape[1] // LINE):
        columns = pl.ds(q * LINE, LINE)
        source = pl.ds(pl.multiple_of(in_quad(q, near) * LINE, LINE), LINE)
        w_copies.append(
            pltpu.make_async_copy(w_hbm.at[:, source], near_ref.at[:, columns], w_sem.at[0, q])
        )
        source = pl.ds(pl.multiple_of(in_quad(q, far) * LINE, LINE), LINE)
        w_copies.append(
            pltpu.make_async_copy(w_hbm.at[half, source], far_ref.at[:, columns], w_sem.at[1, q])
        )
    for copy in k_copies + v_copies + w_copies:
        copy.start()

    q = q_ref[...].astype(F32)
    q_rows = jnp.concatenate(
        [q[:, h * size : (h + 1) * size] for h in range(QUERY_HEADS)], axis=0
    )
    q_lanes = q_rows.T.astype(BF16)
    count = rows * QUERY_HEADS
    lane = lax.broadcasted_iota(jnp.int32, (size, count), 1)
    by_key = [
        jnp.where(lane // (count // KVH) == k, q_lanes, jnp.zeros_like(q_lanes))
        for k in range(KVH)
    ]
    request = lax.broadcasted_iota(jnp.int32, (CTX, count), 1) % rows
    position = lax.broadcasted_iota(jnp.int32, (CTX, count), 0)
    spread = jnp.concatenate(by_key, axis=0)
    scores = jnp.zeros((CTX, count), F32)
    length = jnp.zeros((CTX, count), jnp.int32)
    for r in range(rows):
        k_copies[r].wait()
        all_lanes = jnp.dot(k_ref[r], spread, preferred_element_type=F32)
        scores = jnp.where(request == r, all_lanes, scores)
        length = jnp.where(request == r, len_ref[r], length)
    live = position < length
    scores = jnp.where(live, scores * (1.0 / math.sqrt(size)), -1e30)
    raw = jnp.where(live, jnp.exp(scores - jnp.max(scores, axis=0, keepdims=True)), 0.0)
    probs = (raw / jnp.sum(raw, axis=0, keepdims=True)).T.astype(BF16)
    owner = lax.broadcasted_iota(jnp.int32, (count, CTX), 0) % rows
    wide = jnp.zeros((count, KVH * size), F32)
    for r in range(rows):
        v_copies[r].wait()
        mine = jnp.where(owner == r, probs, jnp.zeros_like(probs))
        wide += jnp.dot(mine, v_ref[r], preferred_element_type=F32)
    group = count // KVH
    own = jnp.concatenate(
        [wide[k * group : (k + 1) * group, k * size : (k + 1) * size] for k in range(KVH)], axis=0
    ).astype(BF16)
    span = QUAD * rows
    for quad in range(QUERY_HEADS // QUAD):
        for m in range(QUAD):
            heads_ref[in_quad(quad, m)] = own[quad * span : (quad + 1) * span]
    for copy in w_copies:
        copy.wait()


def start(place, lengths, queries, key_cache, value_cache, weight):
    rows = queries.shape[0]
    depth, columns = weight.shape
    span = columns // QUAD
    cache = pltpu.VMEM((rows, CTX, KVH * HEAD_SIZE), BF16)
    return pl.pallas_call(
        start_kernel,
        out_shape=(
            jax.ShapeDtypeStruct((QUERY_HEADS, QUAD * rows, HEAD_SIZE), BF16),
            jax.ShapeDtypeStruct((depth, span), BF16),
            jax.ShapeDtypeStruct((depth // 2, span), BF16),
        ),
        in_specs=[SMEM, SMEM, VMEM, HBM, HBM, HBM],
        out_specs=(VMEM,) * 3,
        scratch_shapes=[cache, cache]
        + [pltpu.SemaphoreType.DMA((rows,))] * 2
        + [pltpu.SemaphoreType.DMA((2, span // LINE))],
        compiler_params=WHOLE,
        name="start",
    )(place, lengths, queries, key_cache, value_cache, weight)


def pick_rows(spans, index):
    count, size = spans.shape
    rows = count // QUAD
    row = lax.broadcasted_iota(jnp.int32, (rows, count), 0)
    column = lax.broadcasted_iota(jnp.int32, (rows, count), 1)
    wanted = (row // 4) * 16 + index * 4 + row % 4
    choice = jnp.where(column == wanted, 1.0, 0.0).astype(BF16)
    return jnp.dot(choice, spans, preferred_element_type=F32).astype(BF16)


def shrink_kernel(
    place_ref, block_ref, adapter_ref, spans_ref, down_hbm, out_ref, down_ref, down_sem
):
    down_copy = pltpu.make_async_copy(down_hbm, down_ref, down_sem)
    down_copy.start()
    half = out_ref.shape[1]
    heads = pick_rows(spans_ref[...], place_ref[0] & (QUAD - 1))
    adapter = adapter_ref[...]
    rank = down_ref.shape[1]
    shrink = jnp.zeros((heads.shape[0], rank), F32)
    down_copy.wait()
    for b in range(down_ref.shape[0]):
        mine = jnp.where(adapter == block_ref[b], heads, jnp.zeros_like(heads))
        shrink += lax.dot_general(
            mine, down_ref[b], (((1,), (1,)), ((), ())), preferred_element_type=F32
        )
    packed = jnp.concatenate([shrink[:half], shrink[half:]], axis=1).astype(BF16)
    for m in range(QUAD):
        out_ref[m] = packed


def shrink_parts(place, spans, down, adapter_col, block_adapter):
    half = spans.shape[0] // QUAD // 2
    down = jnp.swapaxes(down, 1, 2)
    return pl.pallas_call(
        shrink_kernel,
        out_shape=jax.ShapeDtypeStruct((QUAD, half, 2 * down.shape[1]), BF16),
        in_specs=[SMEM, SMEM, VMEM, VMEM, HBM],
        out_specs=VMEM,
        scratch_shapes=[pltpu.VMEM(down.shape, BF16), pltpu.SemaphoreType.DMA],
        compiler_params=PARAMS,
        cost_estimate=pl.CostEstimate(flops=6*10**9, bytes_accessed=2**20, transcendentals=0),
        name="shrink",
    )(place, block_adapter, adapter_col, spans, down)


def arrange_kernel(place_ref, spans_ref, out_ref):
    spans = spans_ref[...]
    member, core = place_ref[0] & (QUAD - 1), lax.div(place_ref[0], QUAD)
    near, other = lax.rem(member + 3 + 2 * core, QUAD), lax.rem(member + 1 + 2 * core, QUAD)
    size = spans.shape[1]
    for i, block in enumerate((member, near, other)):
        out_ref[:, i * size : (i + 1) * size] = pick_rows(spans, block)
    opposite = pick_rows(spans, lax.rem(member + 2, QUAD))
    turned = jnp.concatenate([opposite[:, size // 2 :], opposite[:, : size // 2]], axis=1)
    out_ref[:, 3 * size :] = jnp.where(core == 0, opposite, turned)


def arrange(place, spans):
    count, size = spans.shape
    return pl.pallas_call(
        arrange_kernel,
        out_shape=jax.ShapeDtypeStruct((count // QUAD, QUAD * size), BF16),
        in_specs=[SMEM, VMEM],
        out_specs=VMEM,
        compiler_params=PARAMS,
        cost_estimate=pl.CostEstimate(flops=2 * 10**10, bytes_accessed=2**18, transcendentals=0),
        name="arrange",
    )(place, spans)


def project_kernel(
    place_ref, heads_ref, weight_ref, near_ref, far_ref, other_hbm, shrink_ref, out_ref, other_ref, sem
):
    dests, _, width = out_ref.shape
    copies = []
    for d in range(dests):
        columns = pl.ds(d * width, width)
        copies.append(
            pltpu.make_async_copy(other_hbm.at[:, columns], other_ref.at[:, columns], sem.at[d])
        )
    for copy in copies:
        copy.start()
    rows = heads_ref.shape[0]
    heads = heads_ref[...]
    member, depth = place_ref[0] & (QUAD - 1), far_ref.shape[0]
    shrink = shrink_ref[0].astype(F32)
    for m in range(1, QUAD):
        shrink += shrink_ref[m].astype(F32)
    half = shrink.shape[0] // 2
    packed = jnp.concatenate([shrink[:half], shrink[half:]], axis=1).astype(BF16)
    for d in range(dests):
        out_ref[d, rows:, :] = packed
    for d in range(dests):
        first = pl.multiple_of(in_quad(d, member) * width, width)
        columns = pl.ds(d * width, width)
        copies[d].wait()
        stacked = jnp.concatenate(
            [
                weight_ref[:, pl.ds(first, width)],
                near_ref[:, columns],
                other_ref[: 2 * depth, columns],
                far_ref[:, columns],
                other_ref[2 * depth :, columns],
            ],
            axis=0,
        )
        out_ref[d, :rows, :] = jnp.dot(heads, stacked, preferred_element_type=F32).astype(BF16)


def project(place, heads, weight, near, far, other, shrinks):
    rows = heads.shape[0]
    dests = near.shape[1] // LINE
    return pl.pallas_call(
        project_kernel,
        out_shape=jax.ShapeDtypeStruct((dests, rows + shrinks.shape[1] // 2, LINE), BF16),
        in_specs=[SMEM] + [VMEM] * 4 + [HBM, VMEM],
        out_specs=VMEM,
        scratch_shapes=[pltpu.VMEM(other.shape, BF16), pltpu.SemaphoreType.DMA((dests,))],
        compiler_params=PARAMS,
        name="project",
    )(place, heads, weight, near, far, other, shrinks)


def mask_kernel(block_ref, adapter_ref, out_ref):
    rank = out_ref.shape[1] // block_ref.shape[0]
    adapter = adapter_ref[...]
    left = lax.broadcasted_iota(jnp.int32, (out_ref.shape[0], 2 * rank), 1) < rank
    for b in range(0, block_ref.shape[0], 2):
        match = jnp.where(left, block_ref[b], block_ref[b + 1]) == adapter
        out_ref[:, b * rank : (b + 2) * rank] = jnp.where(match, 1.0, 0.0).astype(BF16)


def mask(adapter_col, block_adapter, rank):
    return pl.pallas_call(
        mask_kernel,
        out_shape=jax.ShapeDtypeStruct((adapter_col.shape[0], block_adapter.shape[0] * rank), BF16),
        in_specs=[SMEM, VMEM],
        out_specs=VMEM,
        compiler_params=PARAMS,
        cost_estimate=pl.CostEstimate(flops=2 * 10**10, bytes_accessed=2**18, transcendentals=0),
        name="mask",
    )(block_adapter, adapter_col)


def finish_kernel(mask_ref, parts_ref, up_ref, out_ref):
    count = parts_ref.shape[0]
    rows, width = out_ref.shape
    blocks, rank, _ = up_ref.shape
    lanes = 2 * rank
    packed = parts_ref[0, rows:, :].astype(F32)
    for s in range(1, count):
        packed += parts_ref[s, rows:, :].astype(F32)
    pair = jnp.concatenate([packed[:, :lanes], packed[:, lanes:]], axis=0)
    turned = jnp.concatenate([pair[:, rank:], pair[:, :rank]], axis=1)
    left = lax.broadcasted_iota(jnp.int32, pair.shape, 1) < rank
    low_rank = jnp.concatenate(
        [jnp.where(left, pair, turned), jnp.where(left, turned, pair)], axis=0
    )
    wide = jnp.concatenate([low_rank.astype(BF16)] * (blocks // 2), axis=1)
    lora = jnp.dot(
        wide * mask_ref[...],
        up_ref[...].reshape(blocks * rank, width),
        preferred_element_type=F32,
    )
    total = parts_ref[0, :rows, :].astype(F32)
    for s in range(1, count):
        total += parts_ref[s, :rows, :].astype(F32)
    out_ref[...] = (total + lora).astype(BF16)


def finish(parts, up, chosen):
    return pl.pallas_call(
        finish_kernel,
        out_shape=jax.ShapeDtypeStruct((chosen.shape[0], parts.shape[2]), BF16),
        in_specs=[VMEM] * 3,
        out_specs=VMEM,
        compiler_params=PARAMS,
        name="finish",
    )(chosen, parts, up)


def per_device(
    reps,
    devices,
    queries,
    key_cache,
    value_cache,
    lengths,
    request_adapter,
    block_adapter,
    output_weight,
    down_factors,
    up_factors,
):
    quads = devices // QUAD
    groups = [[in_quad(q, m) for q in range(quads)] for m in range(QUAD)]
    lines = [[in_quad(q, m) for m in range(QUAD)] for q in range(quads)]
    exchange = functools.partial(
        lax.all_to_all, axis_name="tp", split_axis=0, concat_axis=0, tiled=True
    )
    rows = request_adapter.shape[0]
    adapter_col = request_adapter[:, None]
    place = (lax.axis_index("tp") & (QUAD - 1)) + (lax.axis_index("rep") & 1) * QUAD
    place = place.astype(jnp.int32)[None]

    own, near, far = start(place, lengths, queries, key_cache, value_cache, output_weight)
    near = lax.ppermute(
        near,
        ("rep", "tp"),
        [
            (r * devices + in_quad(q, m), r * devices + in_quad(q, (m + 1 + 2 * (r & 1)) % QUAD))
            for r in range(reps)
            for q in range(quads)
            for m in range(QUAD)
        ],
    )
    far = lax.ppermute(
        far, "tp", [(in_quad(q, m), in_quad(q, (m + 2) % QUAD)) for q in range(quads) for m in range(QUAD)]
    )
    spans = exchange(own).reshape(QUAD * rows, HEAD_SIZE)
    partial = shrink_parts(place, spans, down_factors, adapter_col, block_adapter)
    shrinks = exchange(partial, axis_index_groups=lines)
    held, _ = lax.optimization_barrier((jnp.concatenate([near, far], axis=0), partial))
    other = lax.ppermute(held, "rep", [(r, r ^ 1) for r in range(reps)])
    heads = arrange(place, spans)
    parts = exchange(
        project(place, heads, output_weight, near, far, other, shrinks), axis_index_groups=groups
    )
    chosen = mask(adapter_col, block_adapter, up_factors.shape[1])
    return finish(parts, up_factors, chosen)


def solution(mesh):
    in_specs = (
        P(("rep", "tp"), None),
        P(("rep", "tp"), None, None),
        P(("rep", "tp"), None, None),
        P(("rep", "tp")),
        P("rep"),
        P("rep"),
        P("tp", None),
        P("rep", "tp", None),
        P("rep", None, "tp"),
    )
    return jax.shard_map(
        functools.partial(per_device, mesh.shape["rep"], mesh.shape["tp"]),
        mesh=mesh,
        in_specs=in_specs,
        out_specs=P("rep", "tp"),
        check_vma=False,
    )
```

```python
import functools
import math

import jax
import jax.numpy as jnp
from jax import lax
from jax.experimental import pallas as pl
from jax.experimental.pallas import tpu as pltpu
from jax.sharding import PartitionSpec as P

HEAD_SIZE = 128
QUERY_HEADS = 32
KVH = 4
CTX = 256
QUAD = 4
LINE = 256
BF16, F32 = jnp.bfloat16, jnp.float32
VMEM = pl.BlockSpec(memory_space=pltpu.VMEM)
SMEM = pl.BlockSpec(memory_space=pltpu.SMEM)
HBM = pl.BlockSpec(memory_space=pltpu.HBM)
PARAMS = pltpu.CompilerParams(vmem_limit_bytes=16 * 1024 * 1024)
WHOLE = pltpu.CompilerParams(vmem_limit_bytes=60 * 1024 * 1024)


def in_quad(q, m):
    return q * QUAD + m


def start_kernel(
    place_ref, len_ref, q_ref, k_hbm, v_hbm, w_hbm, heads_ref, near_ref, far_ref, k_ref, v_ref, k_sem, v_sem, w_sem
):
    rows, size = k_ref.shape[0], HEAD_SIZE
    k_copies = [pltpu.make_async_copy(k_hbm.at[r], k_ref.at[r], k_sem.at[r]) for r in range(rows)]
    v_copies = [pltpu.make_async_copy(v_hbm.at[r], v_ref.at[r], v_sem.at[r]) for r in range(rows)]
    member, core = place_ref[0] & (QUAD - 1), lax.div(place_ref[0], QUAD)
    near = lax.rem(member + 1 + 2 * core, QUAD)
    far = lax.rem(member + 2, QUAD)
    depth = far_ref.shape[0]
    half = pl.ds(pl.multiple_of(core * depth, depth), depth)
    w_copies = []
    for q in range(near_ref.shape[1] // LINE):
        columns = pl.ds(q * LINE, LINE)
        source = pl.ds(pl.multiple_of(in_quad(q, near) * LINE, LINE), LINE)
        w_copies.append(
            pltpu.make_async_copy(w_hbm.at[:, source], near_ref.at[:, columns], w_sem.at[0, q])
        )
        source = pl.ds(pl.multiple_of(in_quad(q, far) * LINE, LINE), LINE)
        w_copies.append(
            pltpu.make_async_copy(w_hbm.at[half, source], far_ref.at[:, columns], w_sem.at[1, q])
        )
    for copy in k_copies + v_copies + w_copies:
        copy.start()

    q = q_ref[...].astype(F32)
    q_rows = jnp.concatenate(
        [q[:, h * size : (h + 1) * size] for h in range(QUERY_HEADS)], axis=0
    )
    q_lanes = q_rows.T.astype(BF16)
    count = rows * QUERY_HEADS
    lane = lax.broadcasted_iota(jnp.int32, (size, count), 1)
    by_key = [
        jnp.where(lane // (count // KVH) == k, q_lanes, jnp.zeros_like(q_lanes))
        for k in range(KVH)
    ]
    request = lax.broadcasted_iota(jnp.int32, (CTX, count), 1) % rows
    position = lax.broadcasted_iota(jnp.int32, (CTX, count), 0)
    spread = jnp.concatenate(by_key, axis=0)
    scores = jnp.zeros((CTX, count), F32)
    length = jnp.zeros((CTX, count), jnp.int32)
    for r in range(rows):
        k_copies[r].wait()
        all_lanes = jnp.dot(k_ref[r], spread, preferred_element_type=F32)
        scores = jnp.where(request == r, all_lanes, scores)
        length = jnp.where(request == r, len_ref[r], length)
    live = position < length
    scores = jnp.where(live, scores * (1.0 / math.sqrt(size)), -1e30)
    raw = jnp.where(live, jnp.exp(scores - jnp.max(scores, axis=0, keepdims=True)), 0.0)
    probs = (raw / jnp.sum(raw, axis=0, keepdims=True)).T.astype(BF16)
    owner = lax.broadcasted_iota(jnp.int32, (count, CTX), 0) % rows
    wide = jnp.zeros((count, KVH * size), F32)
    for r in range(rows):
        v_copies[r].wait()
        mine = jnp.where(owner == r, probs, jnp.zeros_like(probs))
        wide += jnp.dot(mine, v_ref[r], preferred_element_type=F32)
    group = count // KVH
    own = jnp.concatenate(
        [wide[k * group : (k + 1) * group, k * size : (k + 1) * size] for k in range(KVH)], axis=0
    ).astype(BF16)
    span = QUAD * rows
    for quad in range(QUERY_HEADS // QUAD):
        for m in range(QUAD):
            heads_ref[in_quad(quad, m)] = own[quad * span : (quad + 1) * span]
    for copy in w_copies:
        copy.wait()


def start(place, lengths, queries, key_cache, value_cache, weight):
    rows = queries.shape[0]
    depth, columns = weight.shape
    span = columns // QUAD
    cache = pltpu.VMEM((rows, CTX, KVH * HEAD_SIZE), BF16)
    return pl.pallas_call(
        start_kernel,
        out_shape=(
            jax.ShapeDtypeStruct((QUERY_HEADS, QUAD * rows, HEAD_SIZE), BF16),
            jax.ShapeDtypeStruct((depth, span), BF16),
            jax.ShapeDtypeStruct((depth // 2, span), BF16),
        ),
        in_specs=[SMEM, SMEM, VMEM, HBM, HBM, HBM],
        out_specs=(VMEM,) * 3,
        scratch_shapes=[cache, cache]
        + [pltpu.SemaphoreType.DMA((rows,))] * 2
        + [pltpu.SemaphoreType.DMA((2, span // LINE))],
        compiler_params=WHOLE,
        name="start",
    )(place, lengths, queries, key_cache, value_cache, weight)


def pick_rows(spans, index):
    count, size = spans.shape
    rows = count // QUAD
    row = lax.broadcasted_iota(jnp.int32, (rows, count), 0)
    column = lax.broadcasted_iota(jnp.int32, (rows, count), 1)
    wanted = (row // 4) * 16 + index * 4 + row % 4
    choice = jnp.where(column == wanted, 1.0, 0.0).astype(BF16)
    return jnp.dot(choice, spans, preferred_element_type=F32).astype(BF16)


def shrink_kernel(place_ref, block_ref, adapter_ref, spans_ref, down_ref, out_ref):
    half = out_ref.shape[1]
    heads = pick_rows(spans_ref[...], place_ref[0] & (QUAD - 1))
    adapter = adapter_ref[...]
    rank = down_ref.shape[1]
    shrink = jnp.zeros((heads.shape[0], rank), F32)
    for b in range(down_ref.shape[0]):
        mine = jnp.where(adapter == block_ref[b], heads, jnp.zeros_like(heads))
        shrink += lax.dot_general(
            mine, down_ref[b], (((1,), (1,)), ((), ())), preferred_element_type=F32
        )
    packed = jnp.concatenate([shrink[:half], shrink[half:]], axis=1).astype(BF16)
    for m in range(QUAD):
        out_ref[m] = packed


def shrink_parts(place, spans, down, adapter_col, block_adapter):
    half = spans.shape[0] // QUAD // 2
    return pl.pallas_call(
        shrink_kernel,
        out_shape=jax.ShapeDtypeStruct((QUAD, half, 2 * down.shape[1]), BF16),
        in_specs=[SMEM, SMEM, VMEM, VMEM, VMEM],
        out_specs=VMEM,
        compiler_params=PARAMS,
        cost_estimate=pl.CostEstimate(flops=10**9, bytes_accessed=2**20, transcendentals=0),
        name="shrink",
    )(place, block_adapter, adapter_col, spans, down)


def prepare_kernel(block_ref, adapter_ref, down_hbm, mask_ref, down_ref, sem):
    copy = pltpu.make_async_copy(down_hbm, down_ref, sem)
    copy.start()
    rank = mask_ref.shape[1] // block_ref.shape[0]
    adapter = adapter_ref[...]
    left = lax.broadcasted_iota(jnp.int32, (mask_ref.shape[0], 2 * rank), 1) < rank
    for b in range(0, block_ref.shape[0], 2):
        match = jnp.where(left, block_ref[b], block_ref[b + 1]) == adapter
        mask_ref[:, b * rank : (b + 2) * rank] = jnp.where(match, 1.0, 0.0).astype(BF16)
    copy.wait()


def prepare(adapter_col, block_adapter, down):
    rows, (blocks, rank, _) = adapter_col.shape[0], down.shape
    return pl.pallas_call(
        prepare_kernel,
        out_shape=(
            jax.ShapeDtypeStruct((rows, blocks * rank), BF16),
            jax.ShapeDtypeStruct(down.shape, BF16),
        ),
        in_specs=[SMEM, VMEM, HBM],
        out_specs=(VMEM, VMEM),
        scratch_shapes=[pltpu.SemaphoreType.DMA],
        compiler_params=PARAMS,
        name="prepare",
    )(block_adapter, adapter_col, down)


def arrange_kernel(place_ref, spans_ref, out_ref):
    spans = spans_ref[...]
    member, core = place_ref[0] & (QUAD - 1), lax.div(place_ref[0], QUAD)
    near, other = lax.rem(member + 3 + 2 * core, QUAD), lax.rem(member + 1 + 2 * core, QUAD)
    size = spans.shape[1]
    for i, block in enumerate((member, near, other)):
        out_ref[:, i * size : (i + 1) * size] = pick_rows(spans, block)
    opposite = pick_rows(spans, lax.rem(member + 2, QUAD))
    turned = jnp.concatenate([opposite[:, size // 2 :], opposite[:, : size // 2]], axis=1)
    out_ref[:, 3 * size :] = jnp.where(core == 0, opposite, turned)


def arrange(place, spans):
    count, size = spans.shape
    return pl.pallas_call(
        arrange_kernel,
        out_shape=jax.ShapeDtypeStruct((count // QUAD, QUAD * size), BF16),
        in_specs=[SMEM, VMEM],
        out_specs=VMEM,
        compiler_params=PARAMS,
        cost_estimate=pl.CostEstimate(flops=2 * 10**10, bytes_accessed=2**18, transcendentals=0),
        name="arrange",
    )(place, spans)


def project_kernel(
    place_ref, heads_ref, weight_ref, held_ref, other_ref, shrink_ref, out_ref
):
    dests, _, width = out_ref.shape
    rows = heads_ref.shape[0]
    heads = heads_ref[...]
    member, depth = place_ref[0] & (QUAD - 1), weight_ref.shape[0]
    for d in range(dests):
        first = pl.multiple_of(in_quad(d, member) * width, width)
        columns = pl.ds(d * width, width)
        stacked = jnp.concatenate(
            [
                weight_ref[:, pl.ds(first, width)],
                held_ref[:depth, columns],
                other_ref[:depth, columns],
                held_ref[depth:, columns],
                other_ref[depth:, columns],
            ],
            axis=0,
        )
        out_ref[d, :rows, :] = jnp.dot(heads, stacked, preferred_element_type=F32).astype(BF16)
    shrink = shrink_ref[0].astype(F32)
    for m in range(1, QUAD):
        shrink += shrink_ref[m].astype(F32)
    half = shrink.shape[0] // 2
    packed = jnp.concatenate([shrink[:half], shrink[half:]], axis=1).astype(BF16)
    for d in range(dests):
        out_ref[d, rows:, :] = packed


def project(place, heads, weight, held, other, shrinks):
    rows = heads.shape[0]
    dests = held.shape[1] // LINE
    return pl.pallas_call(
        project_kernel,
        out_shape=jax.ShapeDtypeStruct((dests, rows + shrinks.shape[1] // 2, LINE), BF16),
        in_specs=[SMEM] + [VMEM] * 5,
        out_specs=VMEM,
        compiler_params=PARAMS,
        name="project",
    )(place, heads, weight, held, other, shrinks)


def finish_kernel(mask_ref, parts_ref, up_ref, out_ref):
    count = parts_ref.shape[0]
    rows, width = out_ref.shape
    blocks, rank, _ = up_ref.shape
    lanes = 2 * rank
    packed = parts_ref[0, rows:, :].astype(F32)
    for s in range(1, count):
        packed += parts_ref[s, rows:, :].astype(F32)
    pair = jnp.concatenate([packed[:, :lanes], packed[:, lanes:]], axis=0)
    turned = jnp.concatenate([pair[:, rank:], pair[:, :rank]], axis=1)
    left = lax.broadcasted_iota(jnp.int32, pair.shape, 1) < rank
    low_rank = jnp.concatenate(
        [jnp.where(left, pair, turned), jnp.where(left, turned, pair)], axis=0
    )
    wide = jnp.concatenate([low_rank.astype(BF16)] * (blocks // 2), axis=1)
    lora = jnp.dot(
        wide * mask_ref[...],
        up_ref[...].reshape(blocks * rank, width),
        preferred_element_type=F32,
    )
    total = parts_ref[0, :rows, :].astype(F32)
    for s in range(1, count):
        total += parts_ref[s, :rows, :].astype(F32)
    out_ref[...] = (total + lora).astype(BF16)


def finish(parts, up, chosen):
    return pl.pallas_call(
        finish_kernel,
        out_shape=jax.ShapeDtypeStruct((chosen.shape[0], parts.shape[2]), BF16),
        in_specs=[VMEM] * 3,
        out_specs=VMEM,
        compiler_params=PARAMS,
        name="finish",
    )(chosen, parts, up)


def per_device(
    reps,
    devices,
    queries,
    key_cache,
    value_cache,
    lengths,
    request_adapter,
    block_adapter,
    output_weight,
    down_factors,
    up_factors,
):
    quads = devices // QUAD
    groups = [[in_quad(q, m) for q in range(quads)] for m in range(QUAD)]
    lines = [[in_quad(q, m) for m in range(QUAD)] for q in range(quads)]
    exchange = functools.partial(
        lax.all_to_all, axis_name="tp", split_axis=0, concat_axis=0, tiled=True
    )
    rows = request_adapter.shape[0]
    adapter_col = request_adapter[:, None]
    place = (lax.axis_index("tp") & (QUAD - 1)) + (lax.axis_index("rep") & 1) * QUAD
    place = place.astype(jnp.int32)[None]

    own, near, far = start(place, lengths, queries, key_cache, value_cache, output_weight)
    near = lax.ppermute(
        near,
        ("rep", "tp"),
        [
            (r * devices + in_quad(q, m), r * devices + in_quad(q, (m + 1 + 2 * (r & 1)) % QUAD))
            for r in range(reps)
            for q in range(quads)
            for m in range(QUAD)
        ],
    )
    far = lax.ppermute(
        far, "tp", [(in_quad(q, m), in_quad(q, (m + 2) % QUAD)) for q in range(quads) for m in range(QUAD)]
    )
    spans = exchange(own).reshape(QUAD * rows, HEAD_SIZE)
    chosen, down = prepare(adapter_col, block_adapter, jnp.swapaxes(down_factors, 1, 2))
    partial = shrink_parts(place, spans, down, adapter_col, block_adapter)
    shrinks = exchange(partial, axis_index_groups=lines)
    held, _ = lax.optimization_barrier((jnp.concatenate([near, far], axis=0), partial))
    other = lax.ppermute(held, "rep", [(r, r ^ 1) for r in range(reps)])
    heads = arrange(place, spans)
    parts = exchange(
        project(place, heads, output_weight, held, other, shrinks), axis_index_groups=groups
    )
    return finish(parts, up_factors, chosen)


def solution(mesh):
    in_specs = (
        P(("rep", "tp"), None),
        P(("rep", "tp"), None, None),
        P(("rep", "tp"), None, None),
        P(("rep", "tp")),
        P("rep"),
        P("rep"),
        P("tp", None),
        P("rep", "tp", None),
        P("rep", None, "tp"),
    )
    return jax.shard_map(
        functools.partial(per_device, mesh.shape["rep"], mesh.shape["tp"]),
        mesh=mesh,
        in_specs=in_specs,
        out_specs=P("rep", "tp"),
        check_vma=False,
    )
```

```python
import functools
import math

import jax
import jax.numpy as jnp
from jax import lax
from jax.experimental import pallas as pl
from jax.experimental.pallas import tpu as pltpu
from jax.sharding import PartitionSpec as P

HEAD_SIZE = 128
QUERY_HEADS = 32
KVH = 4
CTX = 256
QUAD = 4
LINE = 256
BF16, F32 = jnp.bfloat16, jnp.float32
VMEM = pl.BlockSpec(memory_space=pltpu.VMEM)
SMEM = pl.BlockSpec(memory_space=pltpu.SMEM)
HBM = pl.BlockSpec(memory_space=pltpu.HBM)
PARAMS = pltpu.CompilerParams(vmem_limit_bytes=16 * 1024 * 1024)
WHOLE = pltpu.CompilerParams(vmem_limit_bytes=60 * 1024 * 1024)


def in_quad(q, m):
    return q * QUAD + m


def start_kernel(
    place_ref, len_ref, q_hbm, k_hbm, v_hbm, w_hbm, heads_ref, near_ref, far_ref, *scratch
):
    q_ref, k_ref, v_ref, q_sem, k_sem, v_sem, w_sem = scratch
    rows, size = k_ref.shape[0], HEAD_SIZE
    k_copies = [pltpu.make_async_copy(k_hbm, k_ref, k_sem)]
    v_copies = [pltpu.make_async_copy(v_hbm, v_ref, v_sem)]
    member, core = place_ref[0] & (QUAD - 1), lax.div(place_ref[0], QUAD)
    near = lax.rem(member + 1 + 2 * core, QUAD)
    far = lax.rem(member + 2, QUAD)
    depth = far_ref.shape[0]
    half = pl.ds(pl.multiple_of(core * depth, depth), depth)
    w_copies = []
    for q in range(near_ref.shape[1] // LINE):
        columns = pl.ds(q * LINE, LINE)
        source = pl.ds(pl.multiple_of(in_quad(q, near) * LINE, LINE), LINE)
        w_copies.append(
            pltpu.make_async_copy(w_hbm.at[:, source], near_ref.at[:, columns], w_sem.at[0, q])
        )
        source = pl.ds(pl.multiple_of(in_quad(q, far) * LINE, LINE), LINE)
        w_copies.append(
            pltpu.make_async_copy(w_hbm.at[half, source], far_ref.at[:, columns], w_sem.at[1, q])
        )
    q_copy = pltpu.make_async_copy(q_hbm, q_ref, q_sem)
    for copy in [q_copy] + k_copies + v_copies:
        copy.start()

    q_copy.wait()
    q = q_ref[...].astype(F32)
    q_rows = jnp.concatenate(
        [q[:, h * size : (h + 1) * size] for h in range(QUERY_HEADS)], axis=0
    )
    q_lanes = q_rows.T.astype(BF16)
    count = rows * QUERY_HEADS
    for copy in w_copies:
        copy.start()
    lane = lax.broadcasted_iota(jnp.int32, (size, count), 1)
    by_key = [
        jnp.where(lane // (count // KVH) == k, q_lanes, jnp.zeros_like(q_lanes))
        for k in range(KVH)
    ]
    request = lax.broadcasted_iota(jnp.int32, (CTX, count), 1) % rows
    position = lax.broadcasted_iota(jnp.int32, (CTX, count), 0)
    spread = jnp.concatenate(by_key, axis=0)
    scores = jnp.zeros((CTX, count), F32)
    length = jnp.zeros((CTX, count), jnp.int32)
    for r in range(rows):
        if r == 0:
            k_copies[0].wait()
        all_lanes = jnp.dot(k_ref[r], spread, preferred_element_type=F32)
        scores = jnp.where(request == r, all_lanes, scores)
        length = jnp.where(request == r, len_ref[r], length)
    live = position < length
    scores = jnp.where(live, scores * (1.0 / math.sqrt(size)), -1e30)
    raw = jnp.where(live, jnp.exp(scores - jnp.max(scores, axis=0, keepdims=True)), 0.0)
    probs = (raw / jnp.sum(raw, axis=0, keepdims=True)).T.astype(BF16)
    owner = lax.broadcasted_iota(jnp.int32, (count, CTX), 0) % rows
    wide = jnp.zeros((count, KVH * size), F32)
    for r in range(rows):
        if r == 0:
            v_copies[0].wait()
        mine = jnp.where(owner == r, probs, jnp.zeros_like(probs))
        wide += jnp.dot(mine, v_ref[r], preferred_element_type=F32)
    group = count // KVH
    own = jnp.concatenate(
        [wide[k * group : (k + 1) * group, k * size : (k + 1) * size] for k in range(KVH)], axis=0
    ).astype(BF16)
    span = QUAD * rows
    for quad in range(QUERY_HEADS // QUAD):
        for m in range(QUAD):
            heads_ref[in_quad(quad, m)] = own[quad * span : (quad + 1) * span]
    for copy in w_copies:
        copy.wait()


def start(place, lengths, queries, key_cache, value_cache, weight):
    rows = queries.shape[0]
    depth, columns = weight.shape
    span = columns // QUAD
    cache = pltpu.VMEM((rows, CTX, KVH * HEAD_SIZE), BF16)
    return pl.pallas_call(
        start_kernel,
        out_shape=(
            jax.ShapeDtypeStruct((QUERY_HEADS, QUAD * rows, HEAD_SIZE), BF16),
            jax.ShapeDtypeStruct((depth, span), BF16),
            jax.ShapeDtypeStruct((depth // 2, span), BF16),
        ),
        in_specs=[SMEM, SMEM, HBM, HBM, HBM, HBM],
        out_specs=(VMEM,) * 3,
        scratch_shapes=[pltpu.VMEM(queries.shape, BF16), cache, cache, pltpu.SemaphoreType.DMA]
        + [pltpu.SemaphoreType.DMA] * 2
        + [pltpu.SemaphoreType.DMA((2, span // LINE))],
        compiler_params=WHOLE,
        name="start",
    )(place, lengths, queries, key_cache, value_cache, weight)


def pick_rows(spans, index):
    count, size = spans.shape
    rows = count // QUAD
    row = lax.broadcasted_iota(jnp.int32, (rows, count), 0)
    column = lax.broadcasted_iota(jnp.int32, (rows, count), 1)
    wanted = (row // 4) * 16 + index * 4 + row % 4
    choice = jnp.where(column == wanted, 1.0, 0.0).astype(BF16)
    return jnp.dot(choice, spans, preferred_element_type=F32).astype(BF16)


def shrink_kernel(place_ref, spans_ref, down_ref, mask_ref, out_ref):
    heads = pick_rows(spans_ref[...], place_ref[0] & (QUAD - 1))
    blocks, rank, depth = down_ref.shape
    every = lax.dot_general(
        heads,
        down_ref[...].reshape(blocks * rank, depth),
        (((1,), (1,)), ((), ())),
        preferred_element_type=F32,
    )
    every = jnp.where(mask_ref[...].astype(F32) > 0, every, 0.0)
    lanes = 2 * rank
    pair = every[:, :lanes]
    for b in range(lanes, blocks * rank, lanes):
        pair += every[:, b : b + lanes]
    twice = pair + jnp.concatenate([pair[:, rank:], pair[:, :rank]], axis=1)
    half = out_ref.shape[1]
    left = lax.broadcasted_iota(jnp.int32, (half, lanes), 1) < rank
    packed = jnp.where(left, twice[:half], twice[half:]).astype(BF16)
    for m in range(QUAD):
        out_ref[m] = packed


def shrink_parts(place, spans, down, chosen):
    half = spans.shape[0] // QUAD // 2
    return pl.pallas_call(
        shrink_kernel,
        out_shape=jax.ShapeDtypeStruct((QUAD, half, 2 * down.shape[1]), BF16),
        in_specs=[SMEM, VMEM, VMEM, VMEM],
        out_specs=VMEM,
        compiler_params=PARAMS,
        cost_estimate=pl.CostEstimate(flops=10**9, bytes_accessed=2**20, transcendentals=0),
        name="shrink",
    )(place, spans, down, chosen)


def prepare_kernel(block_ref, adapter_ref, down_hbm, mask_ref, down_ref, sem):
    copy = pltpu.make_async_copy(down_hbm, down_ref, sem)
    copy.start()
    rank = mask_ref.shape[1] // block_ref.shape[0]
    adapter = adapter_ref[...]
    left = lax.broadcasted_iota(jnp.int32, (mask_ref.shape[0], 2 * rank), 1) < rank
    for b in range(0, block_ref.shape[0], 2):
        match = jnp.where(left, block_ref[b], block_ref[b + 1]) == adapter
        mask_ref[:, b * rank : (b + 2) * rank] = jnp.where(match, 1.0, 0.0).astype(BF16)
    copy.wait()


def prepare(adapter_col, block_adapter, down):
    rows, (blocks, rank, _) = adapter_col.shape[0], down.shape
    return pl.pallas_call(
        prepare_kernel,
        out_shape=(
            jax.ShapeDtypeStruct((rows, blocks * rank), BF16),
            jax.ShapeDtypeStruct(down.shape, BF16),
        ),
        in_specs=[SMEM, VMEM, HBM],
        out_specs=(VMEM, VMEM),
        scratch_shapes=[pltpu.SemaphoreType.DMA],
        compiler_params=PARAMS,
        name="prepare",
    )(block_adapter, adapter_col, down)


def arrange_kernel(place_ref, spans_ref, out_ref):
    spans = spans_ref[...]
    member, core = place_ref[0] & (QUAD - 1), lax.div(place_ref[0], QUAD)
    near, other = lax.rem(member + 3 + 2 * core, QUAD), lax.rem(member + 1 + 2 * core, QUAD)
    size = spans.shape[1]
    for i, block in enumerate((member, near, other)):
        out_ref[:, i * size : (i + 1) * size] = pick_rows(spans, block)
    opposite = pick_rows(spans, lax.rem(member + 2, QUAD))
    turned = jnp.concatenate([opposite[:, size // 2 :], opposite[:, : size // 2]], axis=1)
    out_ref[:, 3 * size :] = jnp.where(core == 0, opposite, turned)


def arrange(place, spans):
    count, size = spans.shape
    return pl.pallas_call(
        arrange_kernel,
        out_shape=jax.ShapeDtypeStruct((count // QUAD, QUAD * size), BF16),
        in_specs=[SMEM, VMEM],
        out_specs=VMEM,
        compiler_params=PARAMS,
        cost_estimate=pl.CostEstimate(flops=2 * 10**10, bytes_accessed=2**18, transcendentals=0),
        name="arrange",
    )(place, spans)


def project_kernel(
    place_ref, heads_ref, weight_ref, held_ref, other_ref, shrink_ref, out_ref
):
    dests, _, width = out_ref.shape
    rows = heads_ref.shape[0]
    heads = heads_ref[...]
    member, depth = place_ref[0] & (QUAD - 1), weight_ref.shape[0]
    for d in range(dests):
        first = pl.multiple_of(in_quad(d, member) * width, width)
        columns = pl.ds(d * width, width)
        stacked = jnp.concatenate(
            [
                weight_ref[:, pl.ds(first, width)],
                held_ref[:depth, columns],
                other_ref[:depth, columns],
                held_ref[depth:, columns],
                other_ref[depth:, columns],
            ],
            axis=0,
        )
        out_ref[d, :rows, :] = jnp.dot(heads, stacked, preferred_element_type=F32).astype(BF16)
    shrink = shrink_ref[0].astype(F32)
    for m in range(1, QUAD):
        shrink += shrink_ref[m].astype(F32)
    half = shrink.shape[0] // 2
    packed = jnp.concatenate([shrink[:half], shrink[half:]], axis=1).astype(BF16)
    for d in range(dests):
        out_ref[d, rows:, :] = packed


def project(place, heads, weight, held, other, shrinks):
    rows = heads.shape[0]
    dests = held.shape[1] // LINE
    return pl.pallas_call(
        project_kernel,
        out_shape=jax.ShapeDtypeStruct((dests, rows + shrinks.shape[1] // 2, LINE), BF16),
        in_specs=[SMEM] + [VMEM] * 5,
        out_specs=VMEM,
        compiler_params=PARAMS,
        name="project",
    )(place, heads, weight, held, other, shrinks)


def finish_kernel(mask_ref, parts_ref, up_ref, out_ref):
    count = parts_ref.shape[0]
    rows, width = out_ref.shape
    blocks, rank, _ = up_ref.shape
    lanes = 2 * rank
    packed = parts_ref[0, rows:, :].astype(F32)
    for s in range(1, count):
        packed += parts_ref[s, rows:, :].astype(F32)
    pair = jnp.concatenate([packed[:, :lanes], packed[:, lanes:]], axis=0)
    turned = jnp.concatenate([pair[:, rank:], pair[:, :rank]], axis=1)
    left = lax.broadcasted_iota(jnp.int32, pair.shape, 1) < rank
    low_rank = jnp.concatenate(
        [jnp.where(left, pair, turned), jnp.where(left, turned, pair)], axis=0
    )
    wide = jnp.concatenate([low_rank.astype(BF16)] * (blocks // 2), axis=1)
    lora = jnp.dot(
        wide * mask_ref[...],
        up_ref[...].reshape(blocks * rank, width),
        preferred_element_type=F32,
    )
    total = parts_ref[0, :rows, :].astype(F32)
    for s in range(1, count):
        total += parts_ref[s, :rows, :].astype(F32)
    out_ref[...] = (total + lora).astype(BF16)


def finish(parts, up, chosen):
    return pl.pallas_call(
        finish_kernel,
        out_shape=jax.ShapeDtypeStruct((chosen.shape[0], parts.shape[2]), BF16),
        in_specs=[VMEM] * 3,
        out_specs=VMEM,
        compiler_params=PARAMS,
        name="finish",
    )(chosen, parts, up)


def per_device(
    reps,
    devices,
    queries,
    key_cache,
    value_cache,
    lengths,
    request_adapter,
    block_adapter,
    output_weight,
    down_factors,
    up_factors,
):
    quads = devices // QUAD
    groups = [[in_quad(q, m) for q in range(quads)] for m in range(QUAD)]
    lines = [[in_quad(q, m) for m in range(QUAD)] for q in range(quads)]
    exchange = functools.partial(
        lax.all_to_all, axis_name="tp", split_axis=0, concat_axis=0, tiled=True
    )
    rows = request_adapter.shape[0]
    adapter_col = request_adapter[:, None]
    place = (lax.axis_index("tp") & (QUAD - 1)) + (lax.axis_index("rep") & 1) * QUAD
    place = place.astype(jnp.int32)[None]

    own, near, far = start(place, lengths, queries, key_cache, value_cache, output_weight)
    near = lax.ppermute(
        near,
        ("rep", "tp"),
        [
            (r * devices + in_quad(q, m), r * devices + in_quad(q, (m + 1 + 2 * (r & 1)) % QUAD))
            for r in range(reps)
            for q in range(quads)
            for m in range(QUAD)
        ],
    )
    far = lax.ppermute(
        far, "tp", [(in_quad(q, m), in_quad(q, (m + 2) % QUAD)) for q in range(quads) for m in range(QUAD)]
    )
    spans = exchange(own).reshape(QUAD * rows, HEAD_SIZE)
    chosen, down = prepare(adapter_col, block_adapter, jnp.swapaxes(down_factors, 1, 2))
    partial = shrink_parts(place, spans, down, chosen)
    shrinks = exchange(partial, axis_index_groups=lines)
    held, _ = lax.optimization_barrier((jnp.concatenate([near, far], axis=0), partial))
    other = lax.ppermute(held, "rep", [(r, r ^ 1) for r in range(reps)])
    heads = arrange(place, spans)
    parts = exchange(
        project(place, heads, output_weight, held, other, shrinks), axis_index_groups=groups
    )
    return finish(parts, up_factors, chosen)


def solution(mesh):
    in_specs = (
        P(("rep", "tp"), None),
        P(("rep", "tp"), None, None),
        P(("rep", "tp"), None, None),
        P(("rep", "tp")),
        P("rep"),
        P("rep"),
        P("tp", None),
        P("rep", "tp", None),
        P("rep", None, "tp"),
    )
    return jax.shard_map(
        functools.partial(per_device, mesh.shape["rep"], mesh.shape["tp"]),
        mesh=mesh,
        in_specs=in_specs,
        out_specs=P("rep", "tp"),
        check_vma=False,
    )
```

```python
import functools
import math

import jax
import jax.numpy as jnp
from jax import lax
from jax.experimental import pallas as pl
from jax.experimental.pallas import tpu as pltpu
from jax.sharding import PartitionSpec as P

HEAD_SIZE = 128
QUERY_HEADS = 32
KVH = 4
CTX = 256
QUAD = 4
LINE = 256
BF16, F32 = jnp.bfloat16, jnp.float32
VMEM = pl.BlockSpec(memory_space=pltpu.VMEM)
SMEM = pl.BlockSpec(memory_space=pltpu.SMEM)
HBM = pl.BlockSpec(memory_space=pltpu.HBM)
PARAMS = pltpu.CompilerParams(vmem_limit_bytes=16 * 1024 * 1024)
WHOLE = pltpu.CompilerParams(vmem_limit_bytes=60 * 1024 * 1024)


def in_quad(q, m):
    return q * QUAD + m


def start_kernel(
    place_ref, len_ref, q_hbm, k_hbm, v_hbm, w_hbm, heads_ref, near_ref, far_ref, *scratch
):
    q_ref, k_ref, v_ref, q_sem, k_sem, v_sem, w_sem = scratch
    rows, size = k_ref.shape[0], HEAD_SIZE
    k_copies = [pltpu.make_async_copy(k_hbm, k_ref, k_sem)]
    v_copies = [pltpu.make_async_copy(v_hbm, v_ref, v_sem)]
    member, core = place_ref[0] & (QUAD - 1), lax.div(place_ref[0], QUAD)
    near = lax.rem(member + 1 + 2 * core, QUAD)
    far = lax.rem(member + 2, QUAD)
    depth = far_ref.shape[0]
    half = pl.ds(pl.multiple_of(core * depth, depth), depth)
    w_copies = []
    for q in range(near_ref.shape[1] // LINE):
        columns = pl.ds(q * LINE, LINE)
        source = pl.ds(pl.multiple_of(in_quad(q, near) * LINE, LINE), LINE)
        w_copies.append(
            pltpu.make_async_copy(w_hbm.at[:, source], near_ref.at[:, columns], w_sem.at[0, q])
        )
        source = pl.ds(pl.multiple_of(in_quad(q, far) * LINE, LINE), LINE)
        w_copies.append(
            pltpu.make_async_copy(w_hbm.at[half, source], far_ref.at[:, columns], w_sem.at[1, q])
        )
    q_copy = pltpu.make_async_copy(q_hbm, q_ref, q_sem)
    for copy in [q_copy] + k_copies + v_copies:
        copy.start()

    q_copy.wait()
    q = q_ref[...].astype(F32)
    q_rows = jnp.concatenate(
        [q[:, h * size : (h + 1) * size] for h in range(QUERY_HEADS)], axis=0
    )
    q_lanes = q_rows.T.astype(BF16)
    count = rows * QUERY_HEADS
    for copy in w_copies:
        copy.start()
    lane = lax.broadcasted_iota(jnp.int32, (size, count), 1)
    by_key = [
        jnp.where(lane // (count // KVH) == k, q_lanes, jnp.zeros_like(q_lanes))
        for k in range(KVH)
    ]
    request = lax.broadcasted_iota(jnp.int32, (CTX, count), 1) % rows
    position = lax.broadcasted_iota(jnp.int32, (CTX, count), 0)
    spread = jnp.concatenate(by_key, axis=0)
    scores = jnp.zeros((CTX, count), F32)
    length = jnp.zeros((CTX, count), jnp.int32)
    for r in range(rows):
        if r == 0:
            k_copies[0].wait()
        all_lanes = jnp.dot(k_ref[r], spread, preferred_element_type=F32)
        scores = jnp.where(request == r, all_lanes, scores)
        length = jnp.where(request == r, len_ref[r], length)
    live = position < length
    scores = jnp.where(live, scores * (1.0 / math.sqrt(size)), -1e30)
    raw = jnp.where(live, jnp.exp(scores - jnp.max(scores, axis=0, keepdims=True)), 0.0)
    probs = (raw / jnp.sum(raw, axis=0, keepdims=True)).T.astype(BF16)
    owner = lax.broadcasted_iota(jnp.int32, (count, CTX), 0) % rows
    wide = jnp.zeros((count, KVH * size), F32)
    for r in range(rows):
        if r == 0:
            v_copies[0].wait()
        mine = jnp.where(owner == r, probs, jnp.zeros_like(probs))
        wide += jnp.dot(mine, v_ref[r], preferred_element_type=F32)
    group = count // KVH
    own = jnp.concatenate(
        [wide[k * group : (k + 1) * group, k * size : (k + 1) * size] for k in range(KVH)], axis=0
    ).astype(BF16)
    span = QUAD * rows
    for quad in range(QUERY_HEADS // QUAD):
        for m in range(QUAD):
            heads_ref[in_quad(quad, m)] = own[quad * span : (quad + 1) * span]
    for copy in w_copies:
        copy.wait()


def start(place, lengths, queries, key_cache, value_cache, weight):
    rows = queries.shape[0]
    depth, columns = weight.shape
    span = columns // QUAD
    cache = pltpu.VMEM((rows, CTX, KVH * HEAD_SIZE), BF16)
    return pl.pallas_call(
        start_kernel,
        out_shape=(
            jax.ShapeDtypeStruct((QUERY_HEADS, QUAD * rows, HEAD_SIZE), BF16),
            jax.ShapeDtypeStruct((depth, span), BF16),
            jax.ShapeDtypeStruct((depth // 2, span), BF16),
        ),
        in_specs=[SMEM, SMEM, HBM, HBM, HBM, HBM],
        out_specs=(VMEM,) * 3,
        scratch_shapes=[pltpu.VMEM(queries.shape, BF16), cache, cache, pltpu.SemaphoreType.DMA]
        + [pltpu.SemaphoreType.DMA] * 2
        + [pltpu.SemaphoreType.DMA((2, span // LINE))],
        compiler_params=WHOLE,
        name="start",
    )(place, lengths, queries, key_cache, value_cache, weight)


def pick_rows(spans, index):
    count, size = spans.shape
    rows = count // QUAD
    row = lax.broadcasted_iota(jnp.int32, (rows, count), 0)
    column = lax.broadcasted_iota(jnp.int32, (rows, count), 1)
    wanted = (row // 4) * 16 + index * 4 + row % 4
    choice = jnp.where(column == wanted, 1.0, 0.0).astype(BF16)
    return jnp.dot(choice, spans, preferred_element_type=F32).astype(BF16)


def shrink_kernel(place_ref, spans_ref, down_ref, mask_ref, out_ref):
    heads = pick_rows(spans_ref[...], place_ref[0] & (QUAD - 1))
    blocks, rank, depth = down_ref.shape
    every = lax.dot_general(
        heads,
        down_ref[...].reshape(blocks * rank, depth),
        (((1,), (1,)), ((), ())),
        preferred_element_type=F32,
    )
    every = jnp.where(mask_ref[...].astype(F32) > 0, every, 0.0)
    lanes = 2 * rank
    pair = every[:, :lanes]
    for b in range(lanes, blocks * rank, lanes):
        pair += every[:, b : b + lanes]
    twice = pair + jnp.concatenate([pair[:, rank:], pair[:, :rank]], axis=1)
    half = out_ref.shape[1]
    left = lax.broadcasted_iota(jnp.int32, (half, lanes), 1) < rank
    packed = jnp.where(left, twice[:half], twice[half:]).astype(BF16)
    for m in range(QUAD):
        out_ref[m] = packed


def shrink_parts(place, spans, down, chosen):
    half = spans.shape[0] // QUAD // 2
    return pl.pallas_call(
        shrink_kernel,
        out_shape=jax.ShapeDtypeStruct((QUAD, half, 2 * down.shape[1]), BF16),
        in_specs=[SMEM, VMEM, VMEM, VMEM],
        out_specs=VMEM,
        compiler_params=PARAMS,
        name="shrink",
    )(place, spans, down, chosen)


def prepare_kernel(block_ref, adapter_ref, down_hbm, mask_ref, down_ref, sem):
    copy = pltpu.make_async_copy(down_hbm, down_ref, sem)
    copy.start()
    rank = mask_ref.shape[1] // block_ref.shape[0]
    adapter = adapter_ref[...]
    left = lax.broadcasted_iota(jnp.int32, (mask_ref.shape[0], 2 * rank), 1) < rank
    for b in range(0, block_ref.shape[0], 2):
        match = jnp.where(left, block_ref[b], block_ref[b + 1]) == adapter
        mask_ref[:, b * rank : (b + 2) * rank] = jnp.where(match, 1.0, 0.0).astype(BF16)
    copy.wait()


def prepare(adapter_col, block_adapter, down):
    rows, (blocks, rank, _) = adapter_col.shape[0], down.shape
    return pl.pallas_call(
        prepare_kernel,
        out_shape=(
            jax.ShapeDtypeStruct((rows, blocks * rank), BF16),
            jax.ShapeDtypeStruct(down.shape, BF16),
        ),
        in_specs=[SMEM, VMEM, HBM],
        out_specs=(VMEM, VMEM),
        scratch_shapes=[pltpu.SemaphoreType.DMA],
        compiler_params=PARAMS,
        name="prepare",
    )(block_adapter, adapter_col, down)


def pass_kernel(held_hbm, after_hbm, out_hbm):
    del held_hbm, after_hbm, out_hbm


def pass_on(held, after):
    return pl.pallas_call(
        pass_kernel,
        out_shape=jax.ShapeDtypeStruct(held.shape, held.dtype),
        in_specs=[HBM] * 2,
        out_specs=HBM,
        input_output_aliases={0: 0},
        compiler_params=PARAMS,
        cost_estimate=pl.CostEstimate(flops=10**10, bytes_accessed=2**18, transcendentals=0),
        name="pass_on",
    )(held, after)


def arrange_kernel(place_ref, spans_ref, out_ref):
    spans = spans_ref[...]
    member, core = place_ref[0] & (QUAD - 1), lax.div(place_ref[0], QUAD)
    near, other = lax.rem(member + 3 + 2 * core, QUAD), lax.rem(member + 1 + 2 * core, QUAD)
    size = spans.shape[1]
    for i, block in enumerate((member, near, other)):
        out_ref[:, i * size : (i + 1) * size] = pick_rows(spans, block)
    opposite = pick_rows(spans, lax.rem(member + 2, QUAD))
    turned = jnp.concatenate([opposite[:, size // 2 :], opposite[:, : size // 2]], axis=1)
    out_ref[:, 3 * size :] = jnp.where(core == 0, opposite, turned)


def arrange(place, spans):
    count, size = spans.shape
    return pl.pallas_call(
        arrange_kernel,
        out_shape=jax.ShapeDtypeStruct((count // QUAD, QUAD * size), BF16),
        in_specs=[SMEM, VMEM],
        out_specs=VMEM,
        compiler_params=PARAMS,
        cost_estimate=pl.CostEstimate(flops=2 * 10**10, bytes_accessed=2**18, transcendentals=0),
        name="arrange",
    )(place, spans)


def project_kernel(
    place_ref, heads_ref, weight_ref, held_ref, other_ref, shrink_ref, out_ref
):
    dests, _, width = out_ref.shape
    rows = heads_ref.shape[0]
    heads = heads_ref[...]
    member, depth = place_ref[0] & (QUAD - 1), weight_ref.shape[0]
    for d in range(dests):
        first = pl.multiple_of(in_quad(d, member) * width, width)
        columns = pl.ds(d * width, width)
        stacked = jnp.concatenate(
            [
                weight_ref[:, pl.ds(first, width)],
                held_ref[:depth, columns],
                other_ref[:depth, columns],
                held_ref[depth:, columns],
                other_ref[depth:, columns],
            ],
            axis=0,
        )
        out_ref[d, :rows, :] = jnp.dot(heads, stacked, preferred_element_type=F32).astype(BF16)
    shrink = shrink_ref[0].astype(F32)
    for m in range(1, QUAD):
        shrink += shrink_ref[m].astype(F32)
    half = shrink.shape[0] // 2
    packed = jnp.concatenate([shrink[:half], shrink[half:]], axis=1).astype(BF16)
    for d in range(dests):
        out_ref[d, rows:, :] = packed


def project(place, heads, weight, held, other, shrinks):
    rows = heads.shape[0]
    dests = held.shape[1] // LINE
    return pl.pallas_call(
        project_kernel,
        out_shape=jax.ShapeDtypeStruct((dests, rows + shrinks.shape[1] // 2, LINE), BF16),
        in_specs=[SMEM] + [VMEM] * 5,
        out_specs=VMEM,
        compiler_params=PARAMS,
        name="project",
    )(place, heads, weight, held, other, shrinks)


def finish_kernel(mask_ref, parts_ref, up_ref, out_ref):
    count = parts_ref.shape[0]
    rows, width = out_ref.shape
    blocks, rank, _ = up_ref.shape
    lanes = 2 * rank
    packed = parts_ref[0, rows:, :].astype(F32)
    for s in range(1, count):
        packed += parts_ref[s, rows:, :].astype(F32)
    pair = jnp.concatenate([packed[:, :lanes], packed[:, lanes:]], axis=0)
    turned = jnp.concatenate([pair[:, rank:], pair[:, :rank]], axis=1)
    left = lax.broadcasted_iota(jnp.int32, pair.shape, 1) < rank
    low_rank = jnp.concatenate(
        [jnp.where(left, pair, turned), jnp.where(left, turned, pair)], axis=0
    )
    wide = jnp.concatenate([low_rank.astype(BF16)] * (blocks // 2), axis=1)
    lora = jnp.dot(
        wide * mask_ref[...],
        up_ref[...].reshape(blocks * rank, width),
        preferred_element_type=F32,
    )
    total = parts_ref[0, :rows, :].astype(F32)
    for s in range(1, count):
        total += parts_ref[s, :rows, :].astype(F32)
    out_ref[...] = (total + lora).astype(BF16)


def finish(parts, up, chosen):
    return pl.pallas_call(
        finish_kernel,
        out_shape=jax.ShapeDtypeStruct((chosen.shape[0], parts.shape[2]), BF16),
        in_specs=[VMEM] * 3,
        out_specs=VMEM,
        compiler_params=PARAMS,
        name="finish",
    )(chosen, parts, up)


def per_device(
    reps,
    devices,
    queries,
    key_cache,
    value_cache,
    lengths,
    request_adapter,
    block_adapter,
    output_weight,
    down_factors,
    up_factors,
):
    quads = devices // QUAD
    groups = [[in_quad(q, m) for q in range(quads)] for m in range(QUAD)]
    lines = [[in_quad(q, m) for m in range(QUAD)] for q in range(quads)]
    exchange = functools.partial(
        lax.all_to_all, axis_name="tp", split_axis=0, concat_axis=0, tiled=True
    )
    rows = request_adapter.shape[0]
    adapter_col = request_adapter[:, None]
    place = (lax.axis_index("tp") & (QUAD - 1)) + (lax.axis_index("rep") & 1) * QUAD
    place = place.astype(jnp.int32)[None]

    own, near, far = start(place, lengths, queries, key_cache, value_cache, output_weight)
    near = lax.ppermute(
        near,
        ("rep", "tp"),
        [
            (r * devices + in_quad(q, m), r * devices + in_quad(q, (m + 1 + 2 * (r & 1)) % QUAD))
            for r in range(reps)
            for q in range(quads)
            for m in range(QUAD)
        ],
    )
    far = lax.ppermute(
        far, "tp", [(in_quad(q, m), in_quad(q, (m + 2) % QUAD)) for q in range(quads) for m in range(QUAD)]
    )
    spans = exchange(own).reshape(QUAD * rows, HEAD_SIZE)
    chosen, down = prepare(adapter_col, block_adapter, jnp.swapaxes(down_factors, 1, 2))
    partial = shrink_parts(place, spans, down, chosen)
    shrinks = exchange(partial, axis_index_groups=lines)
    far = pass_on(far, partial)
    held, _ = lax.optimization_barrier((jnp.concatenate([near, far], axis=0), partial))
    other = lax.ppermute(held, "rep", [(r, r ^ 1) for r in range(reps)])
    heads = arrange(place, spans)
    parts = exchange(
        project(place, heads, output_weight, held, other, shrinks), axis_index_groups=groups
    )
    return finish(parts, up_factors, chosen)


def solution(mesh):
    in_specs = (
        P(("rep", "tp"), None),
        P(("rep", "tp"), None, None),
        P(("rep", "tp"), None, None),
        P(("rep", "tp")),
        P("rep"),
        P("rep"),
        P("tp", None),
        P("rep", "tp", None),
        P("rep", None, "tp"),
    )
    return jax.shard_map(
        functools.partial(per_device, mesh.shape["rep"], mesh.shape["tp"]),
        mesh=mesh,
        in_specs=in_specs,
        out_specs=P("rep", "tp"),
        check_vma=False,
    )
```

```python
import functools
import math

import jax
import jax.numpy as jnp
from jax import lax
from jax.experimental import pallas as pl
from jax.experimental.pallas import tpu as pltpu
from jax.sharding import PartitionSpec as P

HEAD_SIZE = 128
QUERY_HEADS = 32
KVH = 4
CTX = 256
QUAD = 4
LINE = 256
BF16, F32 = jnp.bfloat16, jnp.float32
VMEM = pl.BlockSpec(memory_space=pltpu.VMEM)
SMEM = pl.BlockSpec(memory_space=pltpu.SMEM)
HBM = pl.BlockSpec(memory_space=pltpu.HBM)
PARAMS = pltpu.CompilerParams(vmem_limit_bytes=16 * 1024 * 1024)
WHOLE = pltpu.CompilerParams(vmem_limit_bytes=60 * 1024 * 1024)


def in_quad(q, m):
    return q * QUAD + m


def start_kernel(
    place_ref, len_ref, q_hbm, k_hbm, v_hbm, w_hbm, heads_ref, near_ref, far_ref, *scratch
):
    q_ref, k_ref, v_ref, q_sem, k_sem, v_sem, w_sem = scratch
    rows, size = k_ref.shape[0], HEAD_SIZE
    k_copies = [pltpu.make_async_copy(k_hbm, k_ref, k_sem)]
    v_copies = [pltpu.make_async_copy(v_hbm, v_ref, v_sem)]
    member, core = place_ref[0] & (QUAD - 1), lax.div(place_ref[0], QUAD)
    near = lax.rem(member + 1 + 2 * core, QUAD)
    far = lax.rem(member + 2, QUAD)
    depth = far_ref.shape[0]
    half = pl.ds(pl.multiple_of(core * depth, depth), depth)
    w_copies = []
    for q in range(near_ref.shape[1] // LINE):
        columns = pl.ds(q * LINE, LINE)
        source = pl.ds(pl.multiple_of(in_quad(q, near) * LINE, LINE), LINE)
        w_copies.append(
            pltpu.make_async_copy(w_hbm.at[:, source], near_ref.at[:, columns], w_sem.at[0, q])
        )
        source = pl.ds(pl.multiple_of(in_quad(q, far) * LINE, LINE), LINE)
        w_copies.append(
            pltpu.make_async_copy(w_hbm.at[half, source], far_ref.at[:, columns], w_sem.at[1, q])
        )
    q_copy = pltpu.make_async_copy(q_hbm, q_ref, q_sem)
    for copy in [q_copy] + k_copies + v_copies:
        copy.start()

    q_copy.wait()
    q = q_ref[...].astype(F32)
    q_rows = jnp.concatenate(
        [q[:, h * size : (h + 1) * size] for h in range(QUERY_HEADS)], axis=0
    )
    q_lanes = q_rows.T.astype(BF16)
    count = rows * QUERY_HEADS
    for copy in w_copies:
        copy.start()
    lane = lax.broadcasted_iota(jnp.int32, (size, count), 1)
    by_key = [
        jnp.where(lane // (count // KVH) == k, q_lanes, jnp.zeros_like(q_lanes))
        for k in range(KVH)
    ]
    request = lax.broadcasted_iota(jnp.int32, (CTX, count), 1) % rows
    position = lax.broadcasted_iota(jnp.int32, (CTX, count), 0)
    spread = jnp.concatenate(by_key, axis=0)
    scores = jnp.zeros((CTX, count), F32)
    length = jnp.zeros((CTX, count), jnp.int32)
    for r in range(rows):
        if r == 0:
            k_copies[0].wait()
        all_lanes = jnp.dot(k_ref[r], spread, preferred_element_type=F32)
        scores = jnp.where(request == r, all_lanes, scores)
        length = jnp.where(request == r, len_ref[r], length)
    live = position < length
    scores = jnp.where(live, scores * (1.0 / math.sqrt(size)), -1e30)
    raw = jnp.where(live, jnp.exp(scores - jnp.max(scores, axis=0, keepdims=True)), 0.0)
    probs = (raw / jnp.sum(raw, axis=0, keepdims=True)).T.astype(BF16)
    owner = lax.broadcasted_iota(jnp.int32, (count, CTX), 0) % rows
    wide = jnp.zeros((count, KVH * size), F32)
    for r in range(rows):
        if r == 0:
            v_copies[0].wait()
        mine = jnp.where(owner == r, probs, jnp.zeros_like(probs))
        wide += jnp.dot(mine, v_ref[r], preferred_element_type=F32)
    group = count // KVH
    own = jnp.concatenate(
        [wide[k * group : (k + 1) * group, k * size : (k + 1) * size] for k in range(KVH)], axis=0
    ).astype(BF16)
    span = QUAD * rows
    for quad in range(QUERY_HEADS // QUAD):
        for m in range(QUAD):
            heads_ref[in_quad(quad, m)] = own[quad * span : (quad + 1) * span]
    for copy in w_copies:
        copy.wait()


def start(place, lengths, queries, key_cache, value_cache, weight):
    rows = queries.shape[0]
    depth, columns = weight.shape
    span = columns // QUAD
    cache = pltpu.VMEM((rows, CTX, KVH * HEAD_SIZE), BF16)
    return pl.pallas_call(
        start_kernel,
        out_shape=(
            jax.ShapeDtypeStruct((QUERY_HEADS, QUAD * rows, HEAD_SIZE), BF16),
            jax.ShapeDtypeStruct((depth, span), BF16),
            jax.ShapeDtypeStruct((depth // 2, span), BF16),
        ),
        in_specs=[SMEM, SMEM, HBM, HBM, HBM, HBM],
        out_specs=(VMEM,) * 3,
        scratch_shapes=[pltpu.VMEM(queries.shape, BF16), cache, cache, pltpu.SemaphoreType.DMA]
        + [pltpu.SemaphoreType.DMA] * 2
        + [pltpu.SemaphoreType.DMA((2, span // LINE))],
        compiler_params=WHOLE,
        name="start",
    )(place, lengths, queries, key_cache, value_cache, weight)


def pick_rows(spans, index):
    count, size = spans.shape
    rows = count // QUAD
    row = lax.broadcasted_iota(jnp.int32, (rows, count), 0)
    column = lax.broadcasted_iota(jnp.int32, (rows, count), 1)
    wanted = (row // 4) * 16 + index * 4 + row % 4
    choice = jnp.where(column == wanted, 1.0, 0.0).astype(BF16)
    return jnp.dot(choice, spans, preferred_element_type=F32).astype(BF16)


def shrink_kernel(place_ref, spans_ref, down_ref, mask_ref, out_ref):
    heads = pick_rows(spans_ref[...], place_ref[0] & (QUAD - 1))
    blocks, rank, depth = down_ref.shape
    every = lax.dot_general(
        heads,
        down_ref[...].reshape(blocks * rank, depth),
        (((1,), (1,)), ((), ())),
        preferred_element_type=F32,
    )
    every = jnp.where(mask_ref[...].astype(F32) > 0, every, 0.0)
    lanes = 2 * rank
    pair = every[:, :lanes]
    for b in range(lanes, blocks * rank, lanes):
        pair += every[:, b : b + lanes]
    twice = pair + jnp.concatenate([pair[:, rank:], pair[:, :rank]], axis=1)
    half = out_ref.shape[1]
    left = lax.broadcasted_iota(jnp.int32, (half, lanes), 1) < rank
    packed = jnp.where(left, twice[:half], twice[half:]).astype(BF16)
    for m in range(QUAD):
        out_ref[m] = packed


def shrink_parts(place, spans, down, chosen):
    half = spans.shape[0] // QUAD // 2
    return pl.pallas_call(
        shrink_kernel,
        out_shape=jax.ShapeDtypeStruct((QUAD, half, 2 * down.shape[1]), BF16),
        in_specs=[SMEM, VMEM, VMEM, VMEM],
        out_specs=VMEM,
        compiler_params=PARAMS,
        name="shrink",
    )(place, spans, down, chosen)


def prepare_kernel(block_ref, adapter_ref, down_hbm, mask_ref, down_ref, sem):
    copy = pltpu.make_async_copy(down_hbm, down_ref, sem)
    copy.start()
    rank = mask_ref.shape[1] // block_ref.shape[0]
    adapter = adapter_ref[...]
    left = lax.broadcasted_iota(jnp.int32, (mask_ref.shape[0], 2 * rank), 1) < rank
    for b in range(0, block_ref.shape[0], 2):
        match = jnp.where(left, block_ref[b], block_ref[b + 1]) == adapter
        mask_ref[:, b * rank : (b + 2) * rank] = jnp.where(match, 1.0, 0.0).astype(BF16)
    copy.wait()


def prepare(adapter_col, block_adapter, down):
    rows, (blocks, rank, _) = adapter_col.shape[0], down.shape
    return pl.pallas_call(
        prepare_kernel,
        out_shape=(
            jax.ShapeDtypeStruct((rows, blocks * rank), BF16),
            jax.ShapeDtypeStruct(down.shape, BF16),
        ),
        in_specs=[SMEM, VMEM, HBM],
        out_specs=(VMEM, VMEM),
        scratch_shapes=[pltpu.SemaphoreType.DMA],
        compiler_params=PARAMS,
        name="prepare",
    )(block_adapter, adapter_col, down)


def pass_kernel(held_hbm, after_hbm, out_hbm):
    del held_hbm, after_hbm, out_hbm


def pass_on(held, after):
    return pl.pallas_call(
        pass_kernel,
        out_shape=jax.ShapeDtypeStruct(held.shape, held.dtype),
        in_specs=[HBM] * 2,
        out_specs=HBM,
        input_output_aliases={0: 0},
        compiler_params=PARAMS,
        cost_estimate=pl.CostEstimate(flops=10**10, bytes_accessed=2**18, transcendentals=0),
        name="pass_on",
    )(held, after)


def arrange_kernel(place_ref, spans_ref, out_ref):
    spans = spans_ref[...]
    member, core = place_ref[0] & (QUAD - 1), lax.div(place_ref[0], QUAD)
    near, other = lax.rem(member + 3 + 2 * core, QUAD), lax.rem(member + 1 + 2 * core, QUAD)
    size = spans.shape[1]
    for i, block in enumerate((member, near, other)):
        out_ref[:, i * size : (i + 1) * size] = pick_rows(spans, block)
    opposite = pick_rows(spans, lax.rem(member + 2, QUAD))
    turned = jnp.concatenate([opposite[:, size // 2 :], opposite[:, : size // 2]], axis=1)
    out_ref[:, 3 * size :] = jnp.where(core == 0, opposite, turned)


def arrange(place, spans):
    count, size = spans.shape
    return pl.pallas_call(
        arrange_kernel,
        out_shape=jax.ShapeDtypeStruct((count // QUAD, QUAD * size), BF16),
        in_specs=[SMEM, VMEM],
        out_specs=VMEM,
        compiler_params=PARAMS,
        cost_estimate=pl.CostEstimate(flops=2 * 10**10, bytes_accessed=2**18, transcendentals=0),
        name="arrange",
    )(place, spans)


def project_kernel(place_ref, heads_ref, weight_ref, held_ref, other_ref, out_ref):
    dests, _, width = out_ref.shape
    rows = heads_ref.shape[0]
    heads = heads_ref[...]
    member, depth = place_ref[0] & (QUAD - 1), weight_ref.shape[0]
    for d in range(dests):
        first = pl.multiple_of(in_quad(d, member) * width, width)
        columns = pl.ds(d * width, width)
        stacked = jnp.concatenate(
            [
                weight_ref[:, pl.ds(first, width)],
                held_ref[:depth, columns],
                other_ref[:depth, columns],
                held_ref[depth:, columns],
                other_ref[depth:, columns],
            ],
            axis=0,
        )
        out_ref[d, :rows, :] = jnp.dot(heads, stacked, preferred_element_type=F32).astype(BF16)


def project(place, heads, weight, held, other, extra):
    rows = heads.shape[0]
    dests = held.shape[1] // LINE
    return pl.pallas_call(
        project_kernel,
        out_shape=jax.ShapeDtypeStruct((dests, rows + extra, LINE), BF16),
        in_specs=[SMEM] + [VMEM] * 4,
        out_specs=VMEM,
        compiler_params=PARAMS,
        cost_estimate=pl.CostEstimate(flops=2**20, bytes_accessed=2**10, transcendentals=0),
        name="project",
    )(place, heads, weight, held, other)


def append_kernel(parts_hbm, shrink_ref, out_ref):
    del parts_hbm
    shrink = shrink_ref[0].astype(F32)
    for m in range(1, QUAD):
        shrink += shrink_ref[m].astype(F32)
    half = shrink.shape[0] // 2
    packed = jnp.concatenate([shrink[:half], shrink[half:]], axis=1).astype(BF16)
    for d in range(out_ref.shape[0]):
        out_ref[d] = packed


def append(parts, shrinks):
    dests, rows, width = parts.shape
    extra = shrinks.shape[1] // 2
    return pl.pallas_call(
        append_kernel,
        out_shape=jax.ShapeDtypeStruct(parts.shape, parts.dtype),
        grid=(1,),
        in_specs=[HBM, VMEM],
        out_specs=pl.BlockSpec((dests, extra, width), lambda i: (0, rows // extra - 1, 0)),
        input_output_aliases={0: 0},
        compiler_params=PARAMS,
        name="append",
    )(parts, shrinks)


def finish_kernel(mask_ref, parts_ref, up_ref, out_ref):
    count = parts_ref.shape[0]
    rows, width = out_ref.shape
    blocks, rank, _ = up_ref.shape
    lanes = 2 * rank
    packed = parts_ref[0, rows:, :].astype(F32)
    for s in range(1, count):
        packed += parts_ref[s, rows:, :].astype(F32)
    pair = jnp.concatenate([packed[:, :lanes], packed[:, lanes:]], axis=0)
    turned = jnp.concatenate([pair[:, rank:], pair[:, :rank]], axis=1)
    left = lax.broadcasted_iota(jnp.int32, pair.shape, 1) < rank
    low_rank = jnp.concatenate(
        [jnp.where(left, pair, turned), jnp.where(left, turned, pair)], axis=0
    )
    wide = jnp.concatenate([low_rank.astype(BF16)] * (blocks // 2), axis=1)
    lora = jnp.dot(
        wide * mask_ref[...],
        up_ref[...].reshape(blocks * rank, width),
        preferred_element_type=F32,
    )
    total = parts_ref[0, :rows, :].astype(F32)
    for s in range(1, count):
        total += parts_ref[s, :rows, :].astype(F32)
    out_ref[...] = (total + lora).astype(BF16)


def finish(parts, up, chosen):
    return pl.pallas_call(
        finish_kernel,
        out_shape=jax.ShapeDtypeStruct((chosen.shape[0], parts.shape[2]), BF16),
        in_specs=[VMEM] * 3,
        out_specs=VMEM,
        compiler_params=PARAMS,
        name="finish",
    )(chosen, parts, up)


def per_device(
    reps,
    devices,
    queries,
    key_cache,
    value_cache,
    lengths,
    request_adapter,
    block_adapter,
    output_weight,
    down_factors,
    up_factors,
):
    quads = devices // QUAD
    groups = [[in_quad(q, m) for q in range(quads)] for m in range(QUAD)]
    lines = [[in_quad(q, m) for m in range(QUAD)] for q in range(quads)]
    exchange = functools.partial(
        lax.all_to_all, axis_name="tp", split_axis=0, concat_axis=0, tiled=True
    )
    rows = request_adapter.shape[0]
    adapter_col = request_adapter[:, None]
    place = (lax.axis_index("tp") & (QUAD - 1)) + (lax.axis_index("rep") & 1) * QUAD
    place = place.astype(jnp.int32)[None]

    own, near, far = start(place, lengths, queries, key_cache, value_cache, output_weight)
    near = lax.ppermute(
        near,
        ("rep", "tp"),
        [
            (r * devices + in_quad(q, m), r * devices + in_quad(q, (m + 1 + 2 * (r & 1)) % QUAD))
            for r in range(reps)
            for q in range(quads)
            for m in range(QUAD)
        ],
    )
    far = lax.ppermute(
        far, "tp", [(in_quad(q, m), in_quad(q, (m + 2) % QUAD)) for q in range(quads) for m in range(QUAD)]
    )
    spans = exchange(own).reshape(QUAD * rows, HEAD_SIZE)
    chosen, down = prepare(adapter_col, block_adapter, jnp.swapaxes(down_factors, 1, 2))
    partial = shrink_parts(place, spans, down, chosen)
    shrinks = exchange(partial, axis_index_groups=lines)
    far = pass_on(far, partial)
    held, _ = lax.optimization_barrier((jnp.concatenate([near, far], axis=0), partial))
    other = lax.ppermute(held, "rep", [(r, r ^ 1) for r in range(reps)])
    heads = arrange(place, spans)
    parts = project(place, heads, output_weight, held, other, partial.shape[1] // 2)
    parts = exchange(append(parts, shrinks), axis_index_groups=groups)
    return finish(parts, up_factors, chosen)


def solution(mesh):
    in_specs = (
        P(("rep", "tp"), None),
        P(("rep", "tp"), None, None),
        P(("rep", "tp"), None, None),
        P(("rep", "tp")),
        P("rep"),
        P("rep"),
        P("tp", None),
        P("rep", "tp", None),
        P("rep", None, "tp"),
    )
    return jax.shard_map(
        functools.partial(per_device, mesh.shape["rep"], mesh.shape["tp"]),
        mesh=mesh,
        in_specs=in_specs,
        out_specs=P("rep", "tp"),
        check_vma=False,
    )
```

```python
import functools
import math

import jax
import jax.numpy as jnp
from jax import lax
from jax.experimental import pallas as pl
from jax.experimental.pallas import tpu as pltpu
from jax.sharding import PartitionSpec as P

HEAD_SIZE = 128
QUERY_HEADS = 32
KVH = 4
CTX = 256
QUAD = 4
LINE = 256
BF16, F32 = jnp.bfloat16, jnp.float32
VMEM = pl.BlockSpec(memory_space=pltpu.VMEM)
SMEM = pl.BlockSpec(memory_space=pltpu.SMEM)
HBM = pl.BlockSpec(memory_space=pltpu.HBM)
PARAMS = pltpu.CompilerParams(vmem_limit_bytes=16 * 1024 * 1024)
WHOLE = pltpu.CompilerParams(vmem_limit_bytes=60 * 1024 * 1024)


def in_quad(q, m):
    return q * QUAD + m


def start_kernel(
    place_ref, len_ref, q_ref, k_hbm, v_hbm, w_hbm, heads_ref, near_ref, far_ref, *scratch
):
    k_ref, v_ref, k_sem, v_sem, w_sem = scratch
    rows, size = k_ref.shape[0], HEAD_SIZE
    k_copies = [pltpu.make_async_copy(k_hbm, k_ref, k_sem)]
    v_copies = [pltpu.make_async_copy(v_hbm, v_ref, v_sem)]
    member, core = place_ref[0] & (QUAD - 1), lax.div(place_ref[0], QUAD)
    near = lax.rem(member + 1 + 2 * core, QUAD)
    far = lax.rem(member + 2, QUAD)
    depth = far_ref.shape[0]
    half = pl.ds(pl.multiple_of(core * depth, depth), depth)
    w_copies = []
    for q in range(near_ref.shape[1] // LINE):
        columns = pl.ds(q * LINE, LINE)
        source = pl.ds(pl.multiple_of(in_quad(q, near) * LINE, LINE), LINE)
        w_copies.append(
            pltpu.make_async_copy(w_hbm.at[:, source], near_ref.at[:, columns], w_sem.at[0, q])
        )
        source = pl.ds(pl.multiple_of(in_quad(q, far) * LINE, LINE), LINE)
        w_copies.append(
            pltpu.make_async_copy(w_hbm.at[half, source], far_ref.at[:, columns], w_sem.at[1, q])
        )
    for copy in k_copies + v_copies:
        copy.start()

    q = q_ref[...].astype(F32)
    q_rows = jnp.concatenate(
        [q[:, h * size : (h + 1) * size] for h in range(QUERY_HEADS)], axis=0
    )
    q_lanes = q_rows.T.astype(BF16)
    count = rows * QUERY_HEADS
    for copy in w_copies:
        copy.start()
    lane = lax.broadcasted_iota(jnp.int32, (size, count), 1)
    by_key = [
        jnp.where(lane // (count // KVH) == k, q_lanes, jnp.zeros_like(q_lanes))
        for k in range(KVH)
    ]
    request = lax.broadcasted_iota(jnp.int32, (CTX, count), 1) % rows
    position = lax.broadcasted_iota(jnp.int32, (CTX, count), 0)
    spread = jnp.concatenate(by_key, axis=0)
    scores = jnp.zeros((CTX, count), F32)
    length = jnp.zeros((CTX, count), jnp.int32)
    for r in range(rows):
        if r == 0:
            k_copies[0].wait()
        all_lanes = jnp.dot(k_ref[r], spread, preferred_element_type=F32)
        scores = jnp.where(request == r, all_lanes, scores)
        length = jnp.where(request == r, len_ref[r], length)
    live = position < length
    scores = jnp.where(live, scores * (1.0 / math.sqrt(size)), -1e30)
    raw = jnp.where(live, jnp.exp(scores - jnp.max(scores, axis=0, keepdims=True)), 0.0)
    probs = (raw / jnp.sum(raw, axis=0, keepdims=True)).T.astype(BF16)
    owner = lax.broadcasted_iota(jnp.int32, (count, CTX), 0) % rows
    wide = jnp.zeros((count, KVH * size), F32)
    for r in range(rows):
        if r == 0:
            v_copies[0].wait()
        mine = jnp.where(owner == r, probs, jnp.zeros_like(probs))
        wide += jnp.dot(mine, v_ref[r], preferred_element_type=F32)
    group = count // KVH
    own = jnp.concatenate(
        [wide[k * group : (k + 1) * group, k * size : (k + 1) * size] for k in range(KVH)], axis=0
    ).astype(BF16)
    span = QUAD * rows
    for quad in range(QUERY_HEADS // QUAD):
        for m in range(QUAD):
            heads_ref[in_quad(quad, m)] = own[quad * span : (quad + 1) * span]
    for copy in w_copies:
        copy.wait()


def start(place, lengths, queries, key_cache, value_cache, weight):
    rows = queries.shape[0]
    depth, columns = weight.shape
    span = columns // QUAD
    cache = pltpu.VMEM((rows, CTX, KVH * HEAD_SIZE), BF16)
    return pl.pallas_call(
        start_kernel,
        out_shape=(
            jax.ShapeDtypeStruct((QUERY_HEADS, QUAD * rows, HEAD_SIZE), BF16),
            jax.ShapeDtypeStruct((depth, span), BF16),
            jax.ShapeDtypeStruct((depth // 2, span), BF16),
        ),
        in_specs=[SMEM, SMEM, VMEM, HBM, HBM, HBM],
        out_specs=(VMEM,) * 3,
        scratch_shapes=[cache, cache]
        + [pltpu.SemaphoreType.DMA] * 2
        + [pltpu.SemaphoreType.DMA((2, span // LINE))],
        compiler_params=WHOLE,
        name="start",
    )(place, lengths, queries, key_cache, value_cache, weight)


def pick_rows(spans, index):
    count, size = spans.shape
    rows = count // QUAD
    row = lax.broadcasted_iota(jnp.int32, (rows, count), 0)
    column = lax.broadcasted_iota(jnp.int32, (rows, count), 1)
    wanted = (row // 4) * 16 + index * 4 + row % 4
    choice = jnp.where(column == wanted, 1.0, 0.0).astype(BF16)
    return jnp.dot(choice, spans, preferred_element_type=F32).astype(BF16)


def shrink_kernel(place_ref, spans_ref, down_ref, mask_ref, out_ref):
    heads = pick_rows(spans_ref[...], place_ref[0] & (QUAD - 1))
    blocks, rank, depth = down_ref.shape
    every = lax.dot_general(
        heads,
        down_ref[...].reshape(blocks * rank, depth),
        (((1,), (1,)), ((), ())),
        preferred_element_type=F32,
    )
    every = jnp.where(mask_ref[...].astype(F32) > 0, every, 0.0)
    lanes = 2 * rank
    pair = every[:, :lanes]
    for b in range(lanes, blocks * rank, lanes):
        pair += every[:, b : b + lanes]
    twice = pair + jnp.concatenate([pair[:, rank:], pair[:, :rank]], axis=1)
    half = out_ref.shape[1]
    left = lax.broadcasted_iota(jnp.int32, (half, lanes), 1) < rank
    packed = jnp.where(left, twice[:half], twice[half:]).astype(BF16)
    for m in range(QUAD):
        out_ref[m] = packed


def shrink_parts(place, spans, down, chosen):
    half = spans.shape[0] // QUAD // 2
    return pl.pallas_call(
        shrink_kernel,
        out_shape=jax.ShapeDtypeStruct((QUAD, half, 2 * down.shape[1]), BF16),
        in_specs=[SMEM, VMEM, VMEM, VMEM],
        out_specs=VMEM,
        compiler_params=PARAMS,
        name="shrink",
    )(place, spans, down, chosen)


def prepare_kernel(block_ref, adapter_ref, down_hbm, mask_ref, down_ref, sem):
    copy = pltpu.make_async_copy(down_hbm, down_ref, sem)
    copy.start()
    rank = mask_ref.shape[1] // block_ref.shape[0]
    adapter = adapter_ref[...]
    left = lax.broadcasted_iota(jnp.int32, (mask_ref.shape[0], 2 * rank), 1) < rank
    for b in range(0, block_ref.shape[0], 2):
        match = jnp.where(left, block_ref[b], block_ref[b + 1]) == adapter
        mask_ref[:, b * rank : (b + 2) * rank] = jnp.where(match, 1.0, 0.0).astype(BF16)
    copy.wait()


def prepare(adapter_col, block_adapter, down):
    rows, (blocks, rank, _) = adapter_col.shape[0], down.shape
    return pl.pallas_call(
        prepare_kernel,
        out_shape=(
            jax.ShapeDtypeStruct((rows, blocks * rank), BF16),
            jax.ShapeDtypeStruct(down.shape, BF16),
        ),
        in_specs=[SMEM, VMEM, HBM],
        out_specs=(VMEM, VMEM),
        scratch_shapes=[pltpu.SemaphoreType.DMA],
        compiler_params=PARAMS,
        name="prepare",
    )(block_adapter, adapter_col, down)


def pass_kernel(held_hbm, after_hbm, out_hbm):
    del held_hbm, after_hbm, out_hbm


def pass_on(held, after):
    return pl.pallas_call(
        pass_kernel,
        out_shape=jax.ShapeDtypeStruct(held.shape, held.dtype),
        in_specs=[HBM] * 2,
        out_specs=HBM,
        input_output_aliases={0: 0},
        compiler_params=PARAMS,
        cost_estimate=pl.CostEstimate(flops=10**10, bytes_accessed=2**18, transcendentals=0),
        name="pass_on",
    )(held, after)


def arrange_kernel(place_ref, spans_ref, out_ref):
    spans = spans_ref[...]
    member, core = place_ref[0] & (QUAD - 1), lax.div(place_ref[0], QUAD)
    near, other = lax.rem(member + 3 + 2 * core, QUAD), lax.rem(member + 1 + 2 * core, QUAD)
    size = spans.shape[1]
    for i, block in enumerate((member, near, other)):
        out_ref[:, i * size : (i + 1) * size] = pick_rows(spans, block)
    opposite = pick_rows(spans, lax.rem(member + 2, QUAD))
    turned = jnp.concatenate([opposite[:, size // 2 :], opposite[:, : size // 2]], axis=1)
    out_ref[:, 3 * size :] = jnp.where(core == 0, opposite, turned)


def arrange(place, spans):
    count, size = spans.shape
    return pl.pallas_call(
        arrange_kernel,
        out_shape=jax.ShapeDtypeStruct((count // QUAD, QUAD * size), BF16),
        in_specs=[SMEM, VMEM],
        out_specs=VMEM,
        compiler_params=PARAMS,
        cost_estimate=pl.CostEstimate(flops=2 * 10**10, bytes_accessed=2**18, transcendentals=0),
        name="arrange",
    )(place, spans)


def project_kernel(place_ref, heads_ref, weight_ref, held_ref, other_ref, out_ref):
    dests, _, width = out_ref.shape
    rows = heads_ref.shape[0]
    heads = heads_ref[...]
    member, depth = place_ref[0] & (QUAD - 1), weight_ref.shape[0]
    for d in range(dests):
        first = pl.multiple_of(in_quad(d, member) * width, width)
        columns = pl.ds(d * width, width)
        stacked = jnp.concatenate(
            [
                weight_ref[:, pl.ds(first, width)],
                held_ref[:depth, columns],
                other_ref[:depth, columns],
                held_ref[depth:, columns],
                other_ref[depth:, columns],
            ],
            axis=0,
        )
        out_ref[d, :rows, :] = jnp.dot(heads, stacked, preferred_element_type=F32).astype(BF16)


def project(place, heads, weight, held, other, extra):
    rows = heads.shape[0]
    dests = held.shape[1] // LINE
    return pl.pallas_call(
        project_kernel,
        out_shape=jax.ShapeDtypeStruct((dests, rows + extra, LINE), BF16),
        in_specs=[SMEM] + [VMEM] * 4,
        out_specs=VMEM,
        compiler_params=PARAMS,
        cost_estimate=pl.CostEstimate(flops=2**20, bytes_accessed=2**10, transcendentals=0),
        name="project",
    )(place, heads, weight, held, other)


def append_kernel(parts_hbm, shrink_ref, out_ref):
    del parts_hbm
    shrink = shrink_ref[0].astype(F32)
    for m in range(1, QUAD):
        shrink += shrink_ref[m].astype(F32)
    half = shrink.shape[0] // 2
    packed = jnp.concatenate([shrink[:half], shrink[half:]], axis=1).astype(BF16)
    for d in range(out_ref.shape[0]):
        out_ref[d] = packed


def append(parts, shrinks):
    dests, rows, width = parts.shape
    extra = shrinks.shape[1] // 2
    return pl.pallas_call(
        append_kernel,
        out_shape=jax.ShapeDtypeStruct(parts.shape, parts.dtype),
        grid=(1,),
        in_specs=[HBM, VMEM],
        out_specs=pl.BlockSpec((dests, extra, width), lambda i: (0, rows // extra - 1, 0)),
        input_output_aliases={0: 0},
        compiler_params=PARAMS,
        name="append",
    )(parts, shrinks)


def finish_kernel(mask_ref, parts_ref, up_ref, out_ref):
    count = parts_ref.shape[0]
    rows, width = out_ref.shape
    blocks, rank, _ = up_ref.shape
    lanes = 2 * rank
    packed = parts_ref[0, rows:, :].astype(F32)
    for s in range(1, count):
        packed += parts_ref[s, rows:, :].astype(F32)
    pair = jnp.concatenate([packed[:, :lanes], packed[:, lanes:]], axis=0)
    turned = jnp.concatenate([pair[:, rank:], pair[:, :rank]], axis=1)
    left = lax.broadcasted_iota(jnp.int32, pair.shape, 1) < rank
    low_rank = jnp.concatenate(
        [jnp.where(left, pair, turned), jnp.where(left, turned, pair)], axis=0
    )
    wide = jnp.concatenate([low_rank.astype(BF16)] * (blocks // 2), axis=1)
    lora = jnp.dot(
        wide * mask_ref[...],
        up_ref[...].reshape(blocks * rank, width),
        preferred_element_type=F32,
    )
    total = parts_ref[0, :rows, :].astype(F32)
    for s in range(1, count):
        total += parts_ref[s, :rows, :].astype(F32)
    out_ref[...] = (total + lora).astype(BF16)


def finish(parts, up, chosen):
    return pl.pallas_call(
        finish_kernel,
        out_shape=jax.ShapeDtypeStruct((chosen.shape[0], parts.shape[2]), BF16),
        in_specs=[VMEM] * 3,
        out_specs=VMEM,
        compiler_params=PARAMS,
        name="finish",
    )(chosen, parts, up)


def per_device(
    reps,
    devices,
    queries,
    key_cache,
    value_cache,
    lengths,
    request_adapter,
    block_adapter,
    output_weight,
    down_factors,
    up_factors,
):
    quads = devices // QUAD
    groups = [[in_quad(q, m) for q in range(quads)] for m in range(QUAD)]
    lines = [[in_quad(q, m) for m in range(QUAD)] for q in range(quads)]
    exchange = functools.partial(
        lax.all_to_all, axis_name="tp", split_axis=0, concat_axis=0, tiled=True
    )
    rows = request_adapter.shape[0]
    adapter_col = request_adapter[:, None]
    place = (lax.axis_index("tp") & (QUAD - 1)) + (lax.axis_index("rep") & 1) * QUAD
    place = place.astype(jnp.int32)[None]

    own, near, far = start(place, lengths, queries, key_cache, value_cache, output_weight)
    near = lax.ppermute(
        near,
        ("rep", "tp"),
        [
            (r * devices + in_quad(q, m), r * devices + in_quad(q, (m + 1 + 2 * (r & 1)) % QUAD))
            for r in range(reps)
            for q in range(quads)
            for m in range(QUAD)
        ],
    )
    far = lax.ppermute(
        far, "tp", [(in_quad(q, m), in_quad(q, (m + 2) % QUAD)) for q in range(quads) for m in range(QUAD)]
    )
    spans = exchange(own).reshape(QUAD * rows, HEAD_SIZE)
    chosen, down = prepare(adapter_col, block_adapter, jnp.swapaxes(down_factors, 1, 2))
    partial = shrink_parts(place, spans, down, chosen)
    shrinks = exchange(partial, axis_index_groups=lines)
    far = pass_on(far, partial)
    held, _ = lax.optimization_barrier((jnp.concatenate([near, far], axis=0), partial))
    other = lax.ppermute(held, "rep", [(r, r ^ 1) for r in range(reps)])
    heads = arrange(place, spans)
    parts = project(place, heads, output_weight, held, other, partial.shape[1] // 2)
    parts = exchange(append(parts, shrinks), axis_index_groups=groups)
    return finish(parts, up_factors, chosen)


def solution(mesh):
    in_specs = (
        P(("rep", "tp"), None),
        P(("rep", "tp"), None, None),
        P(("rep", "tp"), None, None),
        P(("rep", "tp")),
        P("rep"),
        P("rep"),
        P("tp", None),
        P("rep", "tp", None),
        P("rep", None, "tp"),
    )
    return jax.shard_map(
        functools.partial(per_device, mesh.shape["rep"], mesh.shape["tp"]),
        mesh=mesh,
        in_specs=in_specs,
        out_specs=P("rep", "tp"),
        check_vma=False,
    )
```

```python
import functools
import math

import jax
import jax.numpy as jnp
from jax import lax
from jax.experimental import pallas as pl
from jax.experimental.pallas import tpu as pltpu
from jax.sharding import PartitionSpec as P

HEAD_SIZE = 128
QUERY_HEADS = 32
KVH = 4
CTX = 256
QUAD = 4
LINE = 256
BF16, F32 = jnp.bfloat16, jnp.float32
VMEM = pl.BlockSpec(memory_space=pltpu.VMEM)
SMEM = pl.BlockSpec(memory_space=pltpu.SMEM)
HBM = pl.BlockSpec(memory_space=pltpu.HBM)
PARAMS = pltpu.CompilerParams(vmem_limit_bytes=16 * 1024 * 1024)
WHOLE = pltpu.CompilerParams(vmem_limit_bytes=60 * 1024 * 1024)


def in_quad(q, m):
    return q * QUAD + m


def start_kernel(
    place_ref, len_ref, q_ref, k_hbm, v_hbm, w_hbm, heads_ref, near_ref, far_ref, *scratch
):
    k_ref, v_ref, k_sem, v_sem, w_sem = scratch
    rows, size = k_ref.shape[0], HEAD_SIZE
    k_copies = [pltpu.make_async_copy(k_hbm, k_ref, k_sem)]
    v_copies = [pltpu.make_async_copy(v_hbm, v_ref, v_sem)]
    member, core = place_ref[0] & (QUAD - 1), lax.div(place_ref[0], QUAD)
    near = lax.rem(member + 1 + 2 * core, QUAD)
    far = lax.rem(member + 2, QUAD)
    depth = far_ref.shape[0]
    half = pl.ds(pl.multiple_of(core * depth, depth), depth)
    w_copies = []
    for q in range(near_ref.shape[1] // LINE):
        columns = pl.ds(q * LINE, LINE)
        source = pl.ds(pl.multiple_of(in_quad(q, near) * LINE, LINE), LINE)
        w_copies.append(
            pltpu.make_async_copy(w_hbm.at[:, source], near_ref.at[:, columns], w_sem.at[0, q])
        )
        source = pl.ds(pl.multiple_of(in_quad(q, far) * LINE, LINE), LINE)
        w_copies.append(
            pltpu.make_async_copy(w_hbm.at[half, source], far_ref.at[:, columns], w_sem.at[1, q])
        )
    for copy in k_copies + v_copies:
        copy.start()

    q = q_ref[...].astype(F32)
    q_rows = jnp.concatenate(
        [q[:, h * size : (h + 1) * size] for h in range(QUERY_HEADS)], axis=0
    )
    q_lanes = q_rows.T.astype(BF16)
    count = rows * QUERY_HEADS
    for copy in w_copies:
        copy.start()
    lane = lax.broadcasted_iota(jnp.int32, (size, count), 1)
    by_key = [
        jnp.where(lane // (count // KVH) == k, q_lanes, jnp.zeros_like(q_lanes))
        for k in range(KVH)
    ]
    request = lax.broadcasted_iota(jnp.int32, (CTX, count), 1) % rows
    position = lax.broadcasted_iota(jnp.int32, (CTX, count), 0)
    spread = jnp.concatenate(by_key, axis=0)
    scores = jnp.zeros((CTX, count), F32)
    length = jnp.zeros((CTX, count), jnp.int32)
    for r in range(rows):
        if r == 0:
            k_copies[0].wait()
        all_lanes = jnp.dot(k_ref[r], spread, preferred_element_type=F32)
        scores = jnp.where(request == r, all_lanes, scores)
        length = jnp.where(request == r, len_ref[r], length)
    live = position < length
    scores = jnp.where(live, scores * (1.0 / math.sqrt(size)), -1e30)
    raw = jnp.where(live, jnp.exp(scores - jnp.max(scores, axis=0, keepdims=True)), 0.0)
    probs = (raw / jnp.sum(raw, axis=0, keepdims=True)).T.astype(BF16)
    owner = lax.broadcasted_iota(jnp.int32, (count, CTX), 0) % rows
    wide = jnp.zeros((count, KVH * size), F32)
    for r in range(rows):
        if r == 0:
            v_copies[0].wait()
        mine = jnp.where(owner == r, probs, jnp.zeros_like(probs))
        wide += jnp.dot(mine, v_ref[r], preferred_element_type=F32)
    group = count // KVH
    own = jnp.concatenate(
        [wide[k * group : (k + 1) * group, k * size : (k + 1) * size] for k in range(KVH)], axis=0
    ).astype(BF16)
    span = QUAD * rows
    for quad in range(QUERY_HEADS // QUAD):
        for m in range(QUAD):
            heads_ref[in_quad(quad, m)] = own[quad * span : (quad + 1) * span]
    for copy in w_copies:
        copy.wait()


def start(place, lengths, queries, key_cache, value_cache, weight):
    rows = queries.shape[0]
    depth, columns = weight.shape
    span = columns // QUAD
    cache = pltpu.VMEM((rows, CTX, KVH * HEAD_SIZE), BF16)
    return pl.pallas_call(
        start_kernel,
        out_shape=(
            jax.ShapeDtypeStruct((QUERY_HEADS, QUAD * rows, HEAD_SIZE), BF16),
            jax.ShapeDtypeStruct((depth, span), BF16),
            jax.ShapeDtypeStruct((depth // 2, span), BF16),
        ),
        in_specs=[SMEM, SMEM, VMEM, HBM, HBM, HBM],
        out_specs=(VMEM,) * 3,
        scratch_shapes=[cache, cache]
        + [pltpu.SemaphoreType.DMA] * 2
        + [pltpu.SemaphoreType.DMA((2, span // LINE))],
        compiler_params=WHOLE,
        name="start",
    )(place, lengths, queries, key_cache, value_cache, weight)


def pick_rows(spans, index):
    count, size = spans.shape
    rows = count // QUAD
    row = lax.broadcasted_iota(jnp.int32, (rows, count), 0)
    column = lax.broadcasted_iota(jnp.int32, (rows, count), 1)
    wanted = (row // 4) * 16 + index * 4 + row % 4
    choice = jnp.where(column == wanted, 1.0, 0.0).astype(BF16)
    return jnp.dot(choice, spans, preferred_element_type=F32).astype(BF16)


def shrink_kernel(place_ref, spans_ref, down_ref, mask_ref, out_ref):
    heads = pick_rows(spans_ref[...], place_ref[0] & (QUAD - 1))
    blocks, rank, depth = down_ref.shape
    every = lax.dot_general(
        heads,
        down_ref[...].reshape(blocks * rank, depth),
        (((1,), (1,)), ((), ())),
        preferred_element_type=F32,
    )
    every = jnp.where(mask_ref[...].astype(F32) > 0, every, 0.0)
    lanes = 2 * rank
    pair = every[:, :lanes]
    for b in range(lanes, blocks * rank, lanes):
        pair += every[:, b : b + lanes]
    twice = pair + jnp.concatenate([pair[:, rank:], pair[:, :rank]], axis=1)
    half = out_ref.shape[1]
    left = lax.broadcasted_iota(jnp.int32, (half, lanes), 1) < rank
    packed = jnp.where(left, twice[:half], twice[half:]).astype(BF16)
    for m in range(QUAD):
        out_ref[m] = packed


def shrink_parts(place, spans, down, chosen):
    half = spans.shape[0] // QUAD // 2
    return pl.pallas_call(
        shrink_kernel,
        out_shape=jax.ShapeDtypeStruct((QUAD, half, 2 * down.shape[1]), BF16),
        in_specs=[SMEM, VMEM, VMEM, VMEM],
        out_specs=VMEM,
        compiler_params=PARAMS,
        cost_estimate=pl.CostEstimate(flops=10**9, bytes_accessed=2**20, transcendentals=0),
        name="shrink",
    )(place, spans, down, chosen)


def prepare_kernel(block_ref, adapter_ref, down_hbm, mask_ref, down_ref, sem):
    copy = pltpu.make_async_copy(down_hbm, down_ref, sem)
    copy.start()
    rank = mask_ref.shape[1] // block_ref.shape[0]
    adapter = adapter_ref[...]
    left = lax.broadcasted_iota(jnp.int32, (mask_ref.shape[0], 2 * rank), 1) < rank
    for b in range(0, block_ref.shape[0], 2):
        match = jnp.where(left, block_ref[b], block_ref[b + 1]) == adapter
        mask_ref[:, b * rank : (b + 2) * rank] = jnp.where(match, 1.0, 0.0).astype(BF16)
    copy.wait()


def prepare(adapter_col, block_adapter, down):
    rows, (blocks, rank, _) = adapter_col.shape[0], down.shape
    return pl.pallas_call(
        prepare_kernel,
        out_shape=(
            jax.ShapeDtypeStruct((rows, blocks * rank), BF16),
            jax.ShapeDtypeStruct(down.shape, BF16),
        ),
        in_specs=[SMEM, VMEM, HBM],
        out_specs=(VMEM, VMEM),
        scratch_shapes=[pltpu.SemaphoreType.DMA],
        compiler_params=PARAMS,
        name="prepare",
    )(block_adapter, adapter_col, down)


def arrange_kernel(place_ref, spans_ref, out_ref):
    spans = spans_ref[...]
    member, core = place_ref[0] & (QUAD - 1), lax.div(place_ref[0], QUAD)
    near, other = lax.rem(member + 3 + 2 * core, QUAD), lax.rem(member + 1 + 2 * core, QUAD)
    size = spans.shape[1]
    for i, block in enumerate((member, near, other)):
        out_ref[:, i * size : (i + 1) * size] = pick_rows(spans, block)
    opposite = pick_rows(spans, lax.rem(member + 2, QUAD))
    turned = jnp.concatenate([opposite[:, size // 2 :], opposite[:, : size // 2]], axis=1)
    out_ref[:, 3 * size :] = jnp.where(core == 0, opposite, turned)


def arrange(place, spans):
    count, size = spans.shape
    return pl.pallas_call(
        arrange_kernel,
        out_shape=jax.ShapeDtypeStruct((count // QUAD, QUAD * size), BF16),
        in_specs=[SMEM, VMEM],
        out_specs=VMEM,
        compiler_params=PARAMS,
        cost_estimate=pl.CostEstimate(flops=2 * 10**10, bytes_accessed=2**18, transcendentals=0),
        name="arrange",
    )(place, spans)


def project_kernel(place_ref, heads_ref, weight_ref, held_ref, other_ref, out_ref):
    dests, _, width = out_ref.shape
    rows = heads_ref.shape[0]
    heads = heads_ref[...]
    member, depth = place_ref[0] & (QUAD - 1), weight_ref.shape[0]
    for d in range(dests):
        first = pl.multiple_of(in_quad(d, member) * width, width)
        columns = pl.ds(d * width, width)
        stacked = jnp.concatenate(
            [
                weight_ref[:, pl.ds(first, width)],
                held_ref[:depth, columns],
                other_ref[:depth, columns],
                held_ref[depth:, columns],
                other_ref[depth:, columns],
            ],
            axis=0,
        )
        out_ref[d, :rows, :] = jnp.dot(heads, stacked, preferred_element_type=F32).astype(BF16)


def project(place, heads, weight, held, other, extra):
    rows = heads.shape[0]
    dests = held.shape[1] // LINE
    return pl.pallas_call(
        project_kernel,
        out_shape=jax.ShapeDtypeStruct((dests, rows + extra, LINE), BF16),
        in_specs=[SMEM] + [VMEM] * 4,
        out_specs=VMEM,
        compiler_params=PARAMS,
        cost_estimate=pl.CostEstimate(flops=2**20, bytes_accessed=2**10, transcendentals=0),
        name="project",
    )(place, heads, weight, held, other)


def append_kernel(parts_hbm, shrink_ref, out_ref):
    del parts_hbm
    shrink = shrink_ref[0].astype(F32)
    for m in range(1, QUAD):
        shrink += shrink_ref[m].astype(F32)
    half = shrink.shape[0] // 2
    packed = jnp.concatenate([shrink[:half], shrink[half:]], axis=1).astype(BF16)
    for d in range(out_ref.shape[0]):
        out_ref[d] = packed


def append(parts, shrinks):
    dests, rows, width = parts.shape
    extra = shrinks.shape[1] // 2
    return pl.pallas_call(
        append_kernel,
        out_shape=jax.ShapeDtypeStruct(parts.shape, parts.dtype),
        grid=(1,),
        in_specs=[HBM, VMEM],
        out_specs=pl.BlockSpec((dests, extra, width), lambda i: (0, rows // extra - 1, 0)),
        input_output_aliases={0: 0},
        compiler_params=PARAMS,
        name="append",
    )(parts, shrinks)


def finish_kernel(mask_ref, parts_ref, up_ref, out_ref):
    count = parts_ref.shape[0]
    rows, width = out_ref.shape
    blocks, rank, _ = up_ref.shape
    lanes = 2 * rank
    packed = parts_ref[0, rows:, :].astype(F32)
    for s in range(1, count):
        packed += parts_ref[s, rows:, :].astype(F32)
    pair = jnp.concatenate([packed[:, :lanes], packed[:, lanes:]], axis=0)
    turned = jnp.concatenate([pair[:, rank:], pair[:, :rank]], axis=1)
    left = lax.broadcasted_iota(jnp.int32, pair.shape, 1) < rank
    low_rank = jnp.concatenate(
        [jnp.where(left, pair, turned), jnp.where(left, turned, pair)], axis=0
    )
    wide = jnp.concatenate([low_rank.astype(BF16)] * (blocks // 2), axis=1)
    lora = jnp.dot(
        wide * mask_ref[...],
        up_ref[...].reshape(blocks * rank, width),
        preferred_element_type=F32,
    )
    total = parts_ref[0, :rows, :].astype(F32)
    for s in range(1, count):
        total += parts_ref[s, :rows, :].astype(F32)
    out_ref[...] = (total + lora).astype(BF16)


def finish(parts, up, chosen):
    return pl.pallas_call(
        finish_kernel,
        out_shape=jax.ShapeDtypeStruct((chosen.shape[0], parts.shape[2]), BF16),
        in_specs=[VMEM] * 3,
        out_specs=VMEM,
        compiler_params=PARAMS,
        name="finish",
    )(chosen, parts, up)


def per_device(
    reps,
    devices,
    queries,
    key_cache,
    value_cache,
    lengths,
    request_adapter,
    block_adapter,
    output_weight,
    down_factors,
    up_factors,
):
    quads = devices // QUAD
    groups = [[in_quad(q, m) for q in range(quads)] for m in range(QUAD)]
    lines = [[in_quad(q, m) for m in range(QUAD)] for q in range(quads)]
    exchange = functools.partial(
        lax.all_to_all, axis_name="tp", split_axis=0, concat_axis=0, tiled=True
    )
    rows = request_adapter.shape[0]
    adapter_col = request_adapter[:, None]
    place = (lax.axis_index("tp") & (QUAD - 1)) + (lax.axis_index("rep") & 1) * QUAD
    place = place.astype(jnp.int32)[None]

    own, near, far = start(place, lengths, queries, key_cache, value_cache, output_weight)
    near = lax.ppermute(
        near,
        ("rep", "tp"),
        [
            (r * devices + in_quad(q, m), r * devices + in_quad(q, (m + 1 + 2 * (r & 1)) % QUAD))
            for r in range(reps)
            for q in range(quads)
            for m in range(QUAD)
        ],
    )
    far = lax.ppermute(
        far, "tp", [(in_quad(q, m), in_quad(q, (m + 2) % QUAD)) for q in range(quads) for m in range(QUAD)]
    )
    spans = exchange(own).reshape(QUAD * rows, HEAD_SIZE)
    chosen, down = prepare(adapter_col, block_adapter, jnp.swapaxes(down_factors, 1, 2))
    partial = shrink_parts(place, spans, down, chosen)
    shrinks = exchange(partial, axis_index_groups=lines)
    held, _ = lax.optimization_barrier((jnp.concatenate([near, far], axis=0), partial))
    other = lax.ppermute(held, "rep", [(r, r ^ 1) for r in range(reps)])
    heads = arrange(place, spans)
    parts = project(place, heads, output_weight, held, other, partial.shape[1] // 2)
    parts = exchange(append(parts, shrinks), axis_index_groups=groups)
    return finish(parts, up_factors, chosen)


def solution(mesh):
    in_specs = (
        P(("rep", "tp"), None),
        P(("rep", "tp"), None, None),
        P(("rep", "tp"), None, None),
        P(("rep", "tp")),
        P("rep"),
        P("rep"),
        P("tp", None),
        P("rep", "tp", None),
        P("rep", None, "tp"),
    )
    return jax.shard_map(
        functools.partial(per_device, mesh.shape["rep"], mesh.shape["tp"]),
        mesh=mesh,
        in_specs=in_specs,
        out_specs=P("rep", "tp"),
        check_vma=False,
    )
```
